256 devices in a mesh: shift: 8 (over z_hi, x), slab: 32 (over z_lo, y, core).
Axes of the slice: x: 4, y: 4, z: 8 (z_hi: 2, z_lo: 4; z = z_hi * 4 + z_lo), core: 2. Of those that a mesh axis runs over, the one named last changes fastest.
Arguments:
- start_state: float32 [256, 8192], P('slab'), may hold values from -6 to 6
- base_field: float32 [256, 8192], P('slab'), may hold values from 1 to 2
- modes: float32 [4, 256, 8192], P(None, 'slab'), may hold values from -0.5 to 0.5
- control: float32 [256, 8192], P('slab'), may hold values from -6 to 6
- target: float32 [256, 8192], P('slab'), may hold values from -12 to 12
- shifts: float32 [8, 4], P('shift'), may hold values from 0 to 1
- gen_vector: int32 [4], replicated, may hold values from 1 to 1020
- point_ids: int32 [4], replicated, may hold values from 0 to 1020
Outputs:
- new_control: float32 [256, 8192], P('slab')
- objective: float32 [], replicated
The draws below stay inside these ranges and needn't reach their ends.
All inputs are finite; a program needn't handle non-finite values.
Results may differ from the reference program's by a relative error of at most 0.0003.
Values sent between devices are 32-bit elements; how exact they have to be, the bound alone decides.
No kernel may reach another device: no remote copies, remote signals or barrier semaphores. Data moves between devices by JAX's collectives and lax.ppermute only.
A program may use at most 64 MiB of HBM per device.

```python
import jax
import jax.numpy as jnp
from jax import lax

COLS = 8192
PTS = 4
MODES = 4
STEPS = 16
NLAT = 1021
NSHIFT = 8
NROWS = 256


def draw_target(key, part):
    key = jax.random.fold_in(key, 7)
    row_pos = jnp.arange(NROWS, dtype=jnp.float32) / max(NROWS - 1, 1)
    ramp = (1.0 + 2.0 * row_pos)[:, None]
    values = jnp.clip(jax.random.normal(key, (NROWS, COLS), jnp.float32), -4.0, 4.0)
    return values * ramp


def with_ends(values, stream_key, low, high):
    spot = [jax.random.randint(jax.random.fold_in(stream_key, axis), (), 0, length) for axis, length in enumerate(values.shape)]
    longest = values.shape.index(max(values.shape))
    next_to = spot[:longest] + [(spot[longest] + 1) % values.shape[longest]] + spot[longest + 1:]
    return values.at[tuple(spot)].set(low).at[tuple(next_to)].set(high)


def level_of(stream_key, dims, split, smallest, largest):
    gain, own = 1.0, jax.random.fold_in(stream_key, 6)
    for dim, parts in split:
        steps = jnp.exp(jax.random.uniform(jax.random.fold_in(own, dim), (parts,), jnp.float32, smallest / len(split), largest / len(split)))
        gain = gain * jnp.repeat(steps, dims[dim] // parts).reshape([-1 if axis == dim else 1 for axis in range(len(dims))])
    return gain


def normal_values(key, extent, scale, bound, pieces=(), held_as=jnp.bfloat16):
    entries = scale * jax.random.normal(key, extent, jnp.float32)
    if pieces:
        entries = entries * level_of(key, extent, pieces, -0.22, 0.18)
    return jnp.clip(entries, -bound, bound).astype(held_as)


def setup_inputs(seed: int = 0) -> dict:
    arg_keys = jax.random.split(jax.random.key(seed), 9)
    start_state = normal_values(arg_keys[0], (NROWS, COLS), 1.0, 6.0, ((0, 32),), jnp.float32)
    base_field = jnp.clip(1.0 + 1.0 * jax.random.uniform(arg_keys[1], (NROWS, COLS), jnp.float32) ** level_of(arg_keys[1], (NROWS, COLS), ((0, 32),), -0.2, 0.2), 1.0, 2.0)
    modes = jnp.clip(jax.random.uniform(arg_keys[2], (MODES, NROWS, COLS), jnp.float32, -0.5, 0.5) * level_of(arg_keys[2], (MODES, NROWS, COLS), ((1, 32),), -0.4, 0.0), -0.5, 0.5)
    control = normal_values(arg_keys[3], (NROWS, COLS), 1.0, 6.0, ((0, 32),), jnp.float32)
    target = draw_target(jax.random.fold_in(arg_keys[8], 71), 0)
    shifts = jnp.clip(1.0 * jax.random.uniform(arg_keys[5], (NSHIFT, MODES), jnp.float32) ** level_of(arg_keys[5], (NSHIFT, MODES), ((0, 8),), -0.2, 0.2), 0.0, 1.0)
    gen_vector = with_ends(jax.random.randint(arg_keys[6], (MODES,), 1, NLAT), jax.random.fold_in(arg_keys[6], 1), 1, NLAT - 1).astype(jnp.int32)
    point_ids = with_ends(jax.random.randint(arg_keys[7], (PTS,), 0, NLAT), jax.random.fold_in(arg_keys[7], 1), 0, NLAT - 1).astype(jnp.int32)
    return {"start_state": start_state, "base_field": base_field, "modes": modes, "control": control, "target": target, "shifts": shifts, "gen_vector": gen_vector, "point_ids": point_ids}


time_step = 0.04
penalty = 0.5
step_length = 0.5

def lattice_weights(gen_vector, point_ids, shift_row):
    product = point_ids[:, None] * gen_vector[None, :] % NLAT
    phases = product.astype(jnp.float32) / NLAT + shift_row[None, :]
    phases = phases - jnp.floor(phases)
    return 0.5 - jnp.abs(2.0 * phases - 1.0)

def apply_step(current, conduct):
    padded = jnp.pad(current, ((0, 0), (1, 1), (1, 1)))
    padded_coef = jnp.pad(conduct, ((0, 0), (1, 1), (1, 1)))
    row_above = padded[:, :-2, 1:-1]
    row_below = padded[:, 2:, 1:-1]
    left_side = padded[:, 1:-1, :-2]
    right_side = padded[:, 1:-1, 2:]
    w_up = 0.5 * (conduct + padded_coef[:, :-2, 1:-1])
    w_down = 0.5 * (conduct + padded_coef[:, 2:, 1:-1])
    w_left = 0.5 * (conduct + padded_coef[:, 1:-1, :-2])
    w_right = 0.5 * (conduct + padded_coef[:, 1:-1, 2:])
    flux_sum = w_up * (row_above - current) + w_down * (row_below - current) + w_left * (left_side - current) + w_right * (right_side - current)
    return current + time_step * flux_sum

def reference(start_state, base_field, modes, control, target, shifts, gen_vector, point_ids):

    def one_shift(shift_row):
        weights = lattice_weights(gen_vector, point_ids, shift_row)
        exponent = jnp.einsum('pk,krc->prc', weights, modes, precision=lax.Precision.HIGHEST)
        conduct = base_field[None] * jnp.exp(exponent)
        states = jnp.broadcast_to(start_state[None], conduct.shape) + jnp.zeros(conduct.shape, jnp.float32)
        states = lax.fori_loop(0, STEPS, lambda counter, current: apply_step(current + time_step * control[None], conduct), states)
        misfit = states - target[None]
        loss_value = 0.5 * jnp.sum(misfit * misfit)

        def adjoint_turn(counter, carry):
            adjoint, running = carry
            adjoint = apply_step(adjoint, conduct)
            return (adjoint, running + adjoint)
        final_adjoint, running = lax.fori_loop(0, STEPS, adjoint_turn, (misfit, jnp.zeros_like(misfit)))
        return (time_step * lax.optimization_barrier(jnp.sum(running, axis=0)), loss_value)
    gradients, losses = lax.map(one_shift, shifts)
    samples = NSHIFT * PTS
    gradient = lax.optimization_barrier(jnp.sum(gradients, axis=0)) / samples + penalty * control
    scaling = step_length / jnp.sqrt(jnp.mean(gradient * gradient) + 1e-06)
    new_control = control - scaling * gradient
    objective = (jnp.sum(losses) / samples + 0.5 * penalty * jnp.sum(control * control)) / (control.shape[0] * control.shape[1])
    return (new_control, objective)
```

```python
import jax
import jax.numpy as jnp
from jax import lax
from jax.experimental import pallas as pl
from jax.experimental.pallas import tpu as pltpu
from jax.sharding import PartitionSpec as P

NLAT = 1021
HALF_DT = 0.02
DT = 0.04
HALO = 32
WIDE = 128
CORE = 64
LINES = 4
BLOCK = 16
LINKS = ("shift", "slab")

def position():
    shift, slab = lax.axis_index("shift"), lax.axis_index("slab")
    z_low, y, core = lax.div(slab, 8), lax.rem(lax.div(slab, 2), 4), lax.rem(slab, 2)
    z_high, x = lax.div(shift, 4), lax.rem(shift, 4)
    block = lax.rem(z_high + lax.div(z_low, 2), 2) * 4 + lax.rem(x - y + 4, 4)
    return block, z_low * 4 + y, core


def device_at(block, place, core):
    z_low, y = divmod(place, 4)
    z_high, x = divmod(block, 4)
    return ((z_high ^ (z_low // 2)) * 4 + (x + y) % 4) * 32 + z_low * 8 + y * 2 + core


BLOCK_GROUPS = [[device_at(b, q, c) for q in range(16)] for b in range(8) for c in range(2)]
CORE_GROUPS = [[device_at(b, q, c) for b in range(8) for q in range(16)] for c in range(2)]
PAIRS = [(i, i ^ 1) for i in range(32)]


def heat_kernel(gen, pts, own, other, part, tall, rows, cond, horiz, diag, mid, cross, cross_up, field, extra, sems):
    lane = lax.broadcasted_iota(jnp.int32, (8, 128), 1)
    sub = lax.broadcasted_iota(jnp.int32, (8, 128), 0)
    half = lane >= 64
    column_block, strip, core = position()
    strip = column_block * 16 + strip
    first_valid = jnp.where(strip == 0, HALO, 0)
    end_valid = jnp.where(strip == 127, WIDE - HALO, WIDE)

    copies = []
    order = (7, 1, 2, 3, 4, 5, 0, 6)
    for a in order:
        pair = [
            pltpu.make_async_copy(own.at[:, a], tall.at[a, :, core], sems.at[a, 0]),
            pltpu.make_async_copy(other.at[:, a], tall.at[a, :, 1 - core], sems.at[a, 1]),
        ]
        for copy in pair:
            copy.start()
        copies.append(pair)
    flat = tall.reshape(8, 256, 128)
    zero = jnp.zeros((8, 128), jnp.float32)
    for i in range(LINES):
        cond[0, i] = zero
        cond[WIDE + 1, i] = zero
        field[0, i] = zero
        field[WIDE + 1, i] = zero
        horiz[0, i] = zero

    for pair, a in zip(copies, order):
        for copy in pair:
            copy.wait()
        for i in range(LINES):
            block = flat[a, pl.ds(i, 64, stride=4), :]
            if a == 6:
                block = DT * block
            if a == 7:
                block = -block
            rows[a, i] = jnp.concatenate([block, block], axis=0).T

    weights = []
    for k in range(4):
        product = [lax.rem(pts[p] * gen[k], NLAT).astype(jnp.float32) / NLAT for p in range(4)]
        value = jnp.where(sub % 4 == 0, product[0], jnp.where(sub % 4 == 1, product[1], jnp.where(sub % 4 == 2, product[2], product[3])))
        found = []
        for y in range(4):
            line = flat[7, pl.ds(core * 128 + 16 * y, 1), :]
            found.append(jnp.broadcast_to(line[:, k : k + 1], (8, 128)))
        shift = jnp.where(half, jnp.where(sub < 4, found[2], found[3]), jnp.where(sub < 4, found[0], found[1]))
        value = value + shift
        value = value - jnp.floor(value)
        weights.append(0.5 - jnp.abs(2.0 * value - 1.0))

    def row(a, i, k):
        return jnp.broadcast_to(rows[a, i, pl.ds(k, 1), :], (8, 128))

    def conduct_at(k, _):
        for i in range(LINES):
            e = (weights[0] * row(2, i, k) + weights[1] * row(3, i, k)) + (weights[2] * row(4, i, k) + weights[3] * row(5, i, k))
            cond[k + 1, i] = row(1, i, k) * jnp.exp(e)
            field[k + 1, i] = row(0, i, k) + row(6, i, k)
        return 0

    lax.fori_loop(0, WIDE, conduct_at, 0, unroll=8)

    top = lane % 64 == 0
    bottom = lane % 64 == 63

    def coefs_at(k, _):
        inside = jnp.logical_and(k >= first_valid, k + 1 < end_valid)
        scale = jnp.where(inside, 1.0, 0.0).astype(jnp.float32)
        c = [HALF_DT * cond[k + 1, i] for i in range(LINES)]
        left = [HALF_DT * cond[k, i] for i in range(LINES)]
        right = [HALF_DT * cond[k + 2, i] for i in range(LINES)]
        up = jnp.where(top, 0.0, pltpu.roll(c[3], 1, 1))
        down = jnp.where(bottom, 0.0, pltpu.roll(c[0], 127, 1))
        edges = [c[0] + up, c[0] + c[1], c[1] + c[2], c[2] + c[3], c[3] + down]
        cross_up[k] = jnp.where(top, 0.0, edges[0])
        for i in range(3):
            mid[k, i] = edges[i + 1]
        cross[k] = jnp.where(bottom, 0.0, edges[4])
        for i in range(LINES):
            toward = c[i] + right[i]
            horiz[k + 1, i] = scale * toward
            diag[k, i] = 1.0 - ((toward + (c[i] + left[i])) + (edges[i] + edges[i + 1]))
        return 0

    lax.fori_loop(0, WIDE, coefs_at, 0, unroll=8)

    def column(k, u, left, right, hl, hr, rolled, source, save):
        r3, r0 = rolled
        m = [mid[k, i] for i in range(3)]
        side = [hl[i] * left[i] + hr[i] * right[i] for i in range(LINES)]
        vert = [
            cross_up[k] * r3 + m[0] * u[1],
            m[0] * u[0] + m[1] * u[2],
            m[1] * u[1] + m[2] * u[3],
            m[2] * u[2] + cross[k] * r0,
        ]
        for i in range(LINES):
            y = (diag[k, i] * u[i] + side[i])
            if source is not None:
                y = y + source(k, i)
            y = y + vert[i]
            field[k + 1, i] = y
            if save:
                extra[k, i] = y

    def load(k):
        return tuple(field[k + 1, i] for i in range(LINES))

    def rolls(u):
        return pltpu.roll(u[3], 1, 1), pltpu.roll(u[0], 127, 1)

    def sweep(low, count, source, save=False):
        def body(block, carry):
            left, u, hl = carry
            base = low + block * BLOCK
            for i in range(BLOCK):
                k = base + i
                right = load(k + 1)
                hr = tuple(horiz[k + 1, j] for j in range(LINES))
                column(k, u, left, right, hl, hr, rolls(u), source, save)
                left, u, hl = u, right, hr
            return (left, u, hl)

        start = (load(low - 1), load(low), tuple(horiz[low, j] for j in range(LINES)))
        lax.fori_loop(0, count // BLOCK, body, start)

    control = lambda k, i: row(6, i, k)
    target = lambda k, i: row(7, i, k)
    misfit = lambda k, i: extra[k, i]

    def columns_of(step):
        return -(-(WIDE - 2 * step) // BLOCK) * BLOCK

    def steps(first, last, source):
        step = first
        while step <= last:
            count = columns_of(step)
            until = step
            while until < last and columns_of(until + 1) == count:
                until += 1

            def one(_, c, count=count):
                sweep((WIDE - count) // 2, count, source)
                return c

            lax.fori_loop(0, until - step + 1, one, 0)
            step = until + 1

    steps(1, 15, control)
    sweep((WIDE - columns_of(16)) // 2, columns_of(16), target, save=True)
    steps(17, 31, misfit)
    sweep((WIDE - columns_of(32)) // 2, columns_of(32), None)

    def add_loss(k, total):
        return tuple(total[i] + extra[k, i] * extra[k, i] for i in range(LINES))

    loss = lax.fori_loop(HALO, HALO + CORE, add_loss, (zero,) * LINES, unroll=8)
    loss = jnp.sum((loss[0] + loss[1]) + (loss[2] + loss[3]), axis=(0, 1), keepdims=True)
    inner = flat[6, :, HALO : HALO + CORE]
    squares = 0.5 * jnp.sum(inner * inner, axis=(0, 1), keepdims=True)
    wide_lane = lax.broadcasted_iota(jnp.int32, (256, CORE), 1)
    part[:, CORE:] = jnp.where(wide_lane == 0, loss, jnp.where(wide_lane == 1, squares, 0.0))
    part[:, :CORE] = 0.25 * inner
    for i in range(LINES):
        total = jnp.sum(field[pl.ds(HALO + 1, CORE), i], axis=1)
        total = (total + pltpu.roll(total, 64, 1)) * (DT / 32)
        part[pl.ds(i, 64, stride=4), :] += jnp.concatenate([total.T[:64], jnp.zeros((64, CORE), jnp.float32)], axis=1)


def heat(gen, pts, own, other):
    smem = pl.BlockSpec(memory_space=pltpu.SMEM)
    vmem = pl.BlockSpec(memory_space=pltpu.VMEM)
    hbm = pl.BlockSpec(memory_space=pl.ANY)
    f32 = jnp.float32
    return pl.pallas_call(
        heat_kernel,
        out_shape=jax.ShapeDtypeStruct((256, 128), f32),
        in_specs=[smem, smem, hbm, hbm],
        out_specs=vmem,
        scratch_shapes=[
            pltpu.VMEM((8, 16, 2, 8, 128), f32),
            pltpu.VMEM((8, LINES, WIDE, 128), f32),
            pltpu.VMEM((WIDE + 2, LINES, 8, 128), f32),
            pltpu.VMEM((WIDE + 1, LINES, 8, 128), f32),
            pltpu.VMEM((WIDE, LINES, 8, 128), f32),
            pltpu.VMEM((WIDE, 3, 8, 128), f32),
            pltpu.VMEM((WIDE, 8, 128), f32),
            pltpu.VMEM((WIDE, 8, 128), f32),
            pltpu.VMEM((WIDE + 2 + BLOCK, LINES, 8, 128), f32),
            pltpu.VMEM((WIDE, LINES, 8, 128), f32),
            pltpu.SemaphoreType.DMA((8, 2)),
        ],
        compiler_params=pltpu.CompilerParams(vmem_limit_bytes=48 * 2**20),
    )(gen, pts, own, other)


def pack_kernel(shifts, start, base, modes, control, target, pieces, window, sems):
    block = position()[0]
    column = pl.multiple_of(block * 1024, 1024)
    before = pl.multiple_of(jnp.maximum(column - 128, 0), 128)
    after = pl.multiple_of(jnp.minimum(column + 1024, 8192 - 128), 128)
    sources = ((start, 0), (base, 1), (control, 6), (target, 7)) + tuple((modes.at[m], 2 + m) for m in range(4))
    copies = []
    for n, (source, a) in enumerate(sources):
        for part, (begin, to, length) in enumerate(((before, 0, 128), (column, 128, 1024), (after, 1152, 128))):
            copy = pltpu.make_async_copy(source.at[:, pl.ds(begin, length)], window.at[a, :, pl.ds(to, length)], sems.at[n, part])
            copy.start()
            copies.append(copy)
    for copy in copies:
        copy.wait()

    @pl.when(block == 0)
    def _():
        window[:, :, :128] = jnp.zeros((8, 8, 128), jnp.float32)

    @pl.when(block == 7)
    def _():
        window[:, :, 1152:] = jnp.zeros((8, 8, 128), jnp.float32)

    lane = lax.broadcasted_iota(jnp.int32, (8, 128), 1)
    vector = jnp.zeros((8, 128), jnp.float32)
    for m in range(4):
        vector = jnp.where(lane == m, shifts[0, m], vector)
    for a in range(8):
        for q in range(16):
            piece = window[a, :, 96 + 64 * q : 224 + 64 * q]
            pieces[q, a] = jnp.where(lane < 4, vector, piece) if a == 7 else piece


def pack(shifts, start, base, modes, control, target):
    hbm = pl.BlockSpec(memory_space=pl.ANY)
    return pl.pallas_call(
        pack_kernel,
        out_shape=jax.ShapeDtypeStruct((16, 8, 8, 128), jnp.float32),
        in_specs=[pl.BlockSpec(memory_space=pltpu.SMEM)] + [hbm] * 5,
        out_specs=pl.BlockSpec(memory_space=pltpu.VMEM),
        scratch_shapes=[pltpu.VMEM((8, 8, 1280), jnp.float32), pltpu.SemaphoreType.DMA((8, 3))],
        compiler_params=pltpu.CompilerParams(vmem_limit_bytes=8 * 2**20),
    )(shifts, start, base, modes, control, target)


def spread_kernel(own, other, pieces, total):
    core = position()[2]
    total[...] = own[...] + other[...]
    lane = lax.broadcasted_iota(jnp.int32, (256, 128), 1)
    gradient = jnp.where(lane < CORE, total[...], 0.0)
    squares = jnp.sum(gradient * gradient, axis=(0, 1), keepdims=True)
    total[...] = jnp.where(lane == CORE + 2, squares, total[...])
    for q in range(16):
        rows = total[pl.ds(pl.multiple_of(16 * q + 8 * core, 8), 8), :]
        for b in range(8):
            pieces[16 * b + q] = rows


def spread(own, other):
    vmem = pl.BlockSpec(memory_space=pltpu.VMEM)
    return pl.pallas_call(
        spread_kernel,
        out_shape=jax.ShapeDtypeStruct((128, 8, 128), jnp.float32),
        in_specs=[vmem, vmem],
        out_specs=vmem,
        scratch_shapes=[pltpu.VMEM((256, 128), jnp.float32)],
        compiler_params=pltpu.CompilerParams(vmem_limit_bytes=8 * 2**20),
    )(own, other)


def finish_kernel(pieces, control, updated, objective):
    lane = lax.broadcasted_iota(jnp.int32, (8, 128), 1)
    sums = [pieces[n] for n in range(128)]
    while len(sums) > 1:
        sums = [a + b for a, b in zip(sums[::2], sums[1::2])]
    stats = sums[0]

    def entry(n):
        return jnp.sum(jnp.where(lane == CORE + n, stats, 0.0)[:1], axis=(0, 1), keepdims=True)

    cells = 256 * 8192
    objective[...] = (entry(0) * (0.5 / 32) + entry(1) * 0.25) / cells
    scaling = jnp.broadcast_to(0.5 / jnp.sqrt(entry(2) / cells + 1e-06), (8, 128))
    for n in range(64):
        gradient = jnp.where(lane < 64, pieces[2 * n], pltpu.roll(pieces[2 * n + 1], 64, 1))
        updated[:, 128 * n : 128 * (n + 1)] = control[:, 128 * n : 128 * (n + 1)] - scaling * gradient


def finish(pieces, control):
    vmem = pl.BlockSpec(memory_space=pltpu.VMEM)
    return pl.pallas_call(
        finish_kernel,
        out_shape=(jax.ShapeDtypeStruct((8, 8192), jnp.float32), jax.ShapeDtypeStruct((1, 1), jnp.float32)),
        in_specs=[vmem, vmem],
        out_specs=(vmem, vmem),
        compiler_params=pltpu.CompilerParams(vmem_limit_bytes=8 * 2**20),
    )(pieces, control)


def local(start_state, base_field, modes, control, target, shifts, gen_vector, point_ids):
    sent = pack(shifts, start_state, base_field, modes, control, target)
    own = lax.all_to_all(sent, LINKS, 0, 0, axis_index_groups=BLOCK_GROUPS, tiled=True)
    other = lax.ppermute(own, "slab", PAIRS)
    part = heat(gen_vector, point_ids, own, other)
    pieces = spread(part, lax.ppermute(part, "slab", PAIRS))
    pieces = lax.all_to_all(pieces, LINKS, 0, 0, axis_index_groups=CORE_GROUPS, tiled=True)
    new_control, objective = finish(pieces, control)
    return new_control, objective[0, 0]


def solution(mesh):
    return jax.shard_map(
        local,
        mesh=mesh,
        in_specs=(
            P("slab", None),
            P("slab", None),
            P(None, "slab", None),
            P("slab", None),
            P("slab", None),
            P("shift", None),
            P(),
            P(),
        ),
        out_specs=(P("slab", None), P()),
        check_vma=False,
    )
```

```python
import jax
import jax.numpy as jnp
from jax import lax
from jax.experimental import pallas as pl
from jax.experimental.pallas import tpu as pltpu
from jax.sharding import PartitionSpec as P

NLAT = 1021
HALF_DT = 0.02
DT = 0.04
HALO = 32
WIDE = 128
CORE = 64
LINES = 4
BLOCK = 43
LINKS = ("shift", "slab")


X_OFF = (2, 1, 0, 1, 3, 2, 3, 0, 3, 0, 3, 2, 0, 1, 2, 1)
X_BITS = sum(x << (2 * q) for q, x in enumerate(X_OFF[:8])), sum(x << (2 * q) for q, x in enumerate(X_OFF[8:]))
SHIFT_ROWS = tuple(tuple(16 * (8 * c + X_OFF[8 * c : 8 * c + 8].index(x)) for x in range(4)) for c in range(2))


def position():
    shift, slab = lax.axis_index("shift"), lax.axis_index("slab")
    z_low, y, core = lax.div(slab, 8), lax.rem(lax.div(slab, 2), 4), lax.rem(slab, 2)
    z_high, x = lax.div(shift, 4), lax.rem(shift, 4)
    place = z_low * 4 + y
    bits = jnp.where(place < 8, X_BITS[0], X_BITS[1])
    offset = lax.rem(lax.shift_right_logical(bits, 2 * lax.rem(place, 8)), 4)
    block = lax.rem(z_high + 1 - lax.div(z_low, 2), 2) * 4 + lax.rem(x - offset + 4, 4)
    return block, place, core


def device_at(block, place, core):
    z_low, y = divmod(place, 4)
    z_high, x = divmod(block, 4)
    return ((z_high ^ (1 - z_low // 2)) * 4 + (x + X_OFF[place]) % 4) * 32 + z_low * 8 + y * 2 + core


BLOCK_GROUPS = [[device_at(b, q, c) for q in range(16)] for b in range(8) for c in range(2)]
CORE_GROUPS = [[device_at(b, q, c) for b in range(8) for q in range(16)] for c in range(2)]
PAIRS = [(i, i ^ 1) for i in range(32)]


def heat_kernel(gen, pts, own, other, part, tall, rows, cond, horiz, ends, mid, cross, field, extra):
    lane = lax.broadcasted_iota(jnp.int32, (8, 128), 1)
    sub = lax.broadcasted_iota(jnp.int32, (8, 128), 0)
    half = lane >= 64
    block, place, core = position()
    strip = block * 16 + place

    for a in range(8):
        for q in range(16):
            tall[a, q, core] = own[q, a]
            tall[a, q, 1 - core] = other[q, a]
    flat = tall.reshape(8, 256, 128)
    zero = jnp.zeros((8, 128), jnp.float32)
    for i in range(LINES):
        cond[0, i] = zero
        cond[WIDE + 1, i] = zero
        field[0, i] = zero
        field[WIDE + 1, i] = zero
        horiz[0, i] = zero
        horiz[WIDE, i] = zero

    for a in range(8):
        for i in range(LINES):
            lines = flat[a, pl.ds(i, 64, stride=4), :]
            if a == 6:
                lines = DT * lines
            if a == 7:
                lines = -lines
            rows[a, i] = jnp.concatenate([lines, lines], axis=0).T

    weights = []
    for k in range(4):
        product = [lax.rem(pts[p] * gen[k], NLAT).astype(jnp.float32) / NLAT for p in range(4)]
        value = jnp.where(sub % 4 == 0, product[0], jnp.where(sub % 4 == 1, product[1], jnp.where(sub % 4 == 2, product[2], product[3])))
        found = []
        for y in range(4):
            line = flat[7, pl.ds(jnp.where(core == 0, SHIFT_ROWS[0][y], SHIFT_ROWS[1][y]), 1), :]
            found.append(jnp.broadcast_to(line[:, k : k + 1], (8, 128)))
        shift = jnp.where(half, jnp.where(sub < 4, found[2], found[3]), jnp.where(sub < 4, found[0], found[1]))
        value = value + shift
        value = value - jnp.floor(value)
        weights.append(0.5 - jnp.abs(2.0 * value - 1.0))

    def row(a, i, k):
        return jnp.broadcast_to(rows[a, i, pl.ds(k, 1), :], (8, 128))

    def conduct_at(k, _):
        for i in range(LINES):
            e = (weights[0] * row(2, i, k) + weights[1] * row(3, i, k)) + (weights[2] * row(4, i, k) + weights[3] * row(5, i, k))
            cond[k + 1, i] = row(1, i, k) * jnp.exp(e)
            field[k + 1, i] = row(0, i, k) + row(6, i, k)
        return 0

    lax.fori_loop(0, WIDE, conduct_at, 0, unroll=8)

    top = lane % 64 == 0
    bottom = lane % 64 == 63

    def coefs_at(k, _):
        c = [HALF_DT * cond[k + 1, i] for i in range(LINES)]
        down = jnp.where(bottom, 0.0, pltpu.roll(c[0], 127, 1))
        for i in range(LINES):
            horiz[k + 1, i] = c[i] + HALF_DT * cond[k + 2, i]
        for i in range(3):
            mid[k, i] = c[i] + c[i + 1]
        cross[k] = jnp.where(bottom, 0.0, c[3] + down)
        ends[k, 0] = jnp.where(top, 1.0 - c[0], 1.0)
        ends[k, 1] = jnp.where(bottom, 1.0 - c[3], 1.0)
        return 0

    lax.fori_loop(0, WIDE, coefs_at, 0, unroll=8)

    def load(k):
        return tuple(field[k + 1, i] for i in range(LINES))

    def flux(k, u, right):
        return tuple(horiz[k + 1, i] * (right[i] - u[i]) for i in range(LINES))

    def sweep(first, last, source, save):
        low, count = first, WIDE - 2 * first
        blocks = -(-count // BLOCK)
        size = -(-count // blocks)

        def body(block, carry):
            before, u = carry
            base = low + block * size
            for n in range(size):
                k = base + n
                right = load(k + 1)
                after = flux(k, u, right)
                down = [mid[k, i] * (u[i + 1] - u[i]) for i in range(3)]
                down.append(cross[k] * (pltpu.roll(u[0], 127, 1) - u[3]))
                wrapped = pltpu.roll(down[3], 1, 1)
                for i in range(LINES):
                    y = (after[i] - before[i]) + (u[i] if 0 < i < 3 else ends[k, i // 3] * u[i])
                    if source is not None:
                        y = y + source(k, i)
                    y = (y + down[i]) - (down[i - 1] if i else wrapped)
                    field[k + 1, i] = y
                    if save:
                        extra[k, i] = y
                before, u = after, right
            return before, u

        u = load(low)
        lax.fori_loop(0, blocks, body, (flux(low - 1, load(low - 1), u), u))

        @pl.when(strip == 0)
        def _():
            for i in range(LINES):
                field[HALO, i] = zero

        @pl.when(strip == 127)
        def _():
            for i in range(LINES):
                field[WIDE - HALO + 1, i] = zero

    def steps(first, last, source, save=False):
        while first <= last:
            until = min(last, first + 3)

            def one(_, c, first=first):
                sweep(first, first, source, save)
                return c

            lax.fori_loop(0, until - first + 1, one, 0)
            first = until + 1

    control = lambda k, i: row(6, i, k)
    target = lambda k, i: row(7, i, k)
    misfit = lambda k, i: extra[k, i]

    steps(1, 15, control)
    steps(16, 16, target, True)

    def add_loss(k, total):
        return tuple(total[i] + extra[k, i] * extra[k, i] for i in range(LINES))

    loss = lax.fori_loop(HALO, HALO + CORE, add_loss, (zero,) * LINES, unroll=8)
    loss = jnp.sum((loss[0] + loss[1]) + (loss[2] + loss[3]), axis=(0, 1), keepdims=True)
    last = 16
    for power in (8, 4, 2, 1):
        steps(last + 1, last + power - 1, None)
        last += power
        steps(last, last, misfit, power > 1)
    steps(32, 32, None)

    inner = flat[6, :, HALO : HALO + CORE]
    squares = 0.5 * jnp.sum(inner * inner, axis=(0, 1), keepdims=True)
    wide_lane = lax.broadcasted_iota(jnp.int32, (256, CORE), 1)
    part[:, CORE:] = jnp.where(wide_lane == 0, loss, jnp.where(wide_lane == 1, squares, 0.0))
    part[:, :CORE] = 0.25 * inner
    for i in range(LINES):
        total = jnp.sum(field[pl.ds(HALO + 1, CORE), i], axis=1)
        total = (total + pltpu.roll(total, 64, 1)) * (DT / 32)
        part[pl.ds(i, 64, stride=4), :] += jnp.concatenate([total.T[:64], jnp.zeros((64, CORE), jnp.float32)], axis=1)


def heat(gen, pts, own, other):
    smem = pl.BlockSpec(memory_space=pltpu.SMEM)
    vmem = pl.BlockSpec(memory_space=pltpu.VMEM)
    f32 = jnp.float32
    return pl.pallas_call(
        heat_kernel,
        out_shape=jax.ShapeDtypeStruct((256, 128), f32),
        in_specs=[smem, smem, vmem, vmem],
        out_specs=vmem,
        scratch_shapes=[
            pltpu.VMEM((8, 16, 2, 8, 128), f32),
            pltpu.VMEM((8, LINES, WIDE, 128), f32),
            pltpu.VMEM((WIDE + 2, LINES, 8, 128), f32),
            pltpu.VMEM((WIDE + 1, LINES, 8, 128), f32),
            pltpu.VMEM((WIDE, 2, 8, 128), f32),
            pltpu.VMEM((WIDE, 3, 8, 128), f32),
            pltpu.VMEM((WIDE, 8, 128), f32),
            pltpu.VMEM((WIDE + 2, LINES, 8, 128), f32),
            pltpu.VMEM((WIDE, LINES, 8, 128), f32),
        ],
        compiler_params=pltpu.CompilerParams(vmem_limit_bytes=48 * 2**20),
    )(gen, pts, own, other)


def pack_kernel(shifts, start, base, modes, control, target, pieces, window, vector_of, sems, sem):
    shift_copy = pltpu.make_async_copy(shifts, vector_of, sem)
    shift_copy.start()
    block = position()[0]
    column = pl.multiple_of(block * 1024, 1024)
    before = pl.multiple_of(jnp.maximum(column - 128, 0), 128)
    after = pl.multiple_of(jnp.minimum(column + 1024, 8192 - 128), 128)
    sources = ((start, 0), (base, 1), (control, 6), (target, 7)) + tuple((modes.at[m], 2 + m) for m in range(4))
    copies = []
    for n, (source, a) in enumerate(sources):
        for part, (begin, to, length) in enumerate(((before, 0, 128), (column, 128, 1024), (after, 1152, 128))):
            copy = pltpu.make_async_copy(source.at[:, pl.ds(begin, length)], window.at[a, :, pl.ds(to, length)], sems.at[n, part])
            copy.start()
            copies.append(copy)
    for copy in copies:
        copy.wait()
    shift_copy.wait()

    @pl.when(block == 0)
    def _():
        window[:, :, :128] = jnp.zeros((8, 8, 128), jnp.float32)

    @pl.when(block == 7)
    def _():
        window[:, :, 1152:] = jnp.zeros((8, 8, 128), jnp.float32)

    lane = lax.broadcasted_iota(jnp.int32, (8, 128), 1)
    vector = jnp.zeros((8, 128), jnp.float32)
    for m in range(4):
        vector = jnp.where(lane == m, vector_of[0, m], vector)
    for a in range(8):
        for q in range(16):
            piece = window[a, :, 96 + 64 * q : 224 + 64 * q]
            pieces[q, a] = jnp.where(lane < 4, vector, piece) if a == 7 else piece


def pack(shifts, start, base, modes, control, target):
    hbm = pl.BlockSpec(memory_space=pltpu.HBM)
    return pl.pallas_call(
        pack_kernel,
        out_shape=jax.ShapeDtypeStruct((16, 8, 8, 128), jnp.float32),
        in_specs=[hbm] * 6,
        out_specs=pl.BlockSpec(memory_space=pltpu.VMEM),
        scratch_shapes=[pltpu.VMEM((8, 8, 1280), jnp.float32), pltpu.SMEM((1, 4), jnp.float32), pltpu.SemaphoreType.DMA((8, 3)), pltpu.SemaphoreType.DMA],
        compiler_params=pltpu.CompilerParams(vmem_limit_bytes=8 * 2**20),
    )(shifts, start, base, modes, control, target)


def spread_kernel(own, other, pieces, total):
    core = position()[2]
    total[...] = own[...] + other[...]
    lane = lax.broadcasted_iota(jnp.int32, (256, 128), 1)
    gradient = jnp.where(lane < CORE, total[...], 0.0)
    squares = jnp.sum(gradient * gradient, axis=(0, 1), keepdims=True)
    total[...] = jnp.where(lane == CORE + 2, squares, total[...])
    for q in range(16):
        rows = total[pl.ds(pl.multiple_of(16 * q + 8 * core, 8), 8), :]
        for b in range(8):
            pieces[16 * b + q] = rows


def spread(own, other):
    vmem = pl.BlockSpec(memory_space=pltpu.VMEM)
    return pl.pallas_call(
        spread_kernel,
        out_shape=jax.ShapeDtypeStruct((128, 8, 128), jnp.float32),
        in_specs=[vmem, vmem],
        out_specs=vmem,
        scratch_shapes=[pltpu.VMEM((256, 128), jnp.float32)],
        compiler_params=pltpu.CompilerParams(vmem_limit_bytes=8 * 2**20),
    )(own, other)


def finish_kernel(pieces, control, updated, objective):
    lane = lax.broadcasted_iota(jnp.int32, (8, 128), 1)
    sums = [pieces[n] for n in range(128)]
    while len(sums) > 1:
        sums = [a + b for a, b in zip(sums[::2], sums[1::2])]
    stats = sums[0]

    def entry(n):
        return jnp.sum(jnp.where(lane == CORE + n, stats, 0.0)[:1], axis=(0, 1), keepdims=True)

    cells = 256 * 8192
    objective[...] = (entry(0) * (0.5 / 32) + entry(1) * 0.25) / cells
    scaling = jnp.broadcast_to(0.5 / jnp.sqrt(entry(2) / cells + 1e-06), (8, 128))
    for n in range(64):
        gradient = jnp.where(lane < 64, pieces[2 * n], pltpu.roll(pieces[2 * n + 1], 64, 1))
        updated[:, 128 * n : 128 * (n + 1)] = control[:, 128 * n : 128 * (n + 1)] - scaling * gradient


def finish(pieces, control):
    vmem = pl.BlockSpec(memory_space=pltpu.VMEM)
    return pl.pallas_call(
        finish_kernel,
        out_shape=(jax.ShapeDtypeStruct((8, 8192), jnp.float32), jax.ShapeDtypeStruct((1, 1), jnp.float32)),
        in_specs=[vmem, vmem],
        out_specs=(vmem, vmem),
        compiler_params=pltpu.CompilerParams(vmem_limit_bytes=8 * 2**20),
    )(pieces, control)


def local(start_state, base_field, modes, control, target, shifts, gen_vector, point_ids):
    sent = pack(shifts, start_state, base_field, modes, control, target)
    own = lax.all_to_all(sent, LINKS, 0, 0, axis_index_groups=BLOCK_GROUPS, tiled=True)
    other = lax.ppermute(own, "slab", PAIRS)
    part = heat(gen_vector, point_ids, own, other)
    pieces = spread(part, lax.ppermute(part, "slab", PAIRS))
    pieces = lax.all_to_all(pieces, LINKS, 0, 0, axis_index_groups=CORE_GROUPS, tiled=True)
    new_control, objective = finish(pieces, control)
    return new_control, objective[0, 0]


def solution(mesh):
    return jax.shard_map(
        local,
        mesh=mesh,
        in_specs=(
            P("slab", None),
            P("slab", None),
            P(None, "slab", None),
            P("slab", None),
            P("slab", None),
            P("shift", None),
            P(),
            P(),
        ),
        out_specs=(P("slab", None), P()),
        check_vma=False,
    )
```

```python
import jax
import jax.numpy as jnp
from jax import lax
from jax.experimental import pallas as pl
from jax.experimental.pallas import tpu as pltpu
from jax.sharding import PartitionSpec as P

NLAT = 1021
HALF_DT = 0.02
DT = 0.04
HALO = 32
WIDE = 128
CORE = 64
LINES = 4
BLOCK = 43
PIECE = 5
LINKS = ("shift", "slab")


X_OFF = (2, 1, 0, 1, 3, 2, 3, 0, 3, 0, 3, 2, 0, 1, 2, 1)
X_BITS = sum(x << (2 * q) for q, x in enumerate(X_OFF[:8])), sum(x << (2 * q) for q, x in enumerate(X_OFF[8:]))
SHIFT_ROWS = tuple(tuple(16 * (8 * c + X_OFF[8 * c : 8 * c + 8].index(x)) for x in range(4)) for c in range(2))


def position():
    shift, slab = lax.axis_index("shift"), lax.axis_index("slab")
    z_low, y, core = lax.div(slab, 8), lax.rem(lax.div(slab, 2), 4), lax.rem(slab, 2)
    z_high, x = lax.div(shift, 4), lax.rem(shift, 4)
    place = z_low * 4 + y
    bits = jnp.where(place < 8, X_BITS[0], X_BITS[1])
    offset = lax.rem(lax.shift_right_logical(bits, 2 * lax.rem(place, 8)), 4)
    block = lax.rem(z_high + 1 - lax.div(z_low, 2), 2) * 4 + lax.rem(x - offset + 4, 4)
    return block, place, core


def device_at(block, place, core):
    z_low, y = divmod(place, 4)
    z_high, x = divmod(block, 4)
    return ((z_high ^ (1 - z_low // 2)) * 4 + (x + X_OFF[place]) % 4) * 32 + z_low * 8 + y * 2 + core


BLOCK_GROUPS = [[device_at(b, q, c) for q in range(16)] for b in range(8) for c in range(2)]
CORE_GROUPS = [[device_at(b, q, c) for b in range(8) for q in range(16)] for c in range(2)]
PAIRS = [(i, i ^ 1) for i in range(32)]


def heat_kernel(gen, pts, own, other, part, tall, rows, cond, horiz, ends, mid, cross, field, extra):
    lane = lax.broadcasted_iota(jnp.int32, (8, 128), 1)
    sub = lax.broadcasted_iota(jnp.int32, (8, 128), 0)
    half = lane >= 64
    block, place, core = position()
    strip = block * 16 + place

    for a in range(8):
        for q in range(16):
            tall[a, q, core] = own[q, a]
            tall[a, q, 1 - core] = other[q, a]
    flat = tall.reshape(8, 256, 128)
    zero = jnp.zeros((8, 128), jnp.float32)
    for i in range(LINES):
        cond[0, i] = zero
        cond[WIDE + 1, i] = zero
        field[0, i] = zero
        field[WIDE + 1, i] = zero
        horiz[0, i] = zero
        horiz[WIDE, i] = zero

    for a in range(8):
        for i in range(LINES):
            lines = flat[a, pl.ds(i, 64, stride=4), :]
            if a == 6:
                lines = DT * lines
            if a == 7:
                lines = -lines
            rows[a, i] = jnp.concatenate([lines, lines], axis=0).T

    weights = []
    for k in range(4):
        product = [lax.rem(pts[p] * gen[k], NLAT).astype(jnp.float32) / NLAT for p in range(4)]
        value = jnp.where(sub % 4 == 0, product[0], jnp.where(sub % 4 == 1, product[1], jnp.where(sub % 4 == 2, product[2], product[3])))
        found = []
        for y in range(4):
            line = flat[7, pl.ds(jnp.where(core == 0, SHIFT_ROWS[0][y], SHIFT_ROWS[1][y]), 1), :]
            found.append(jnp.broadcast_to(line[:, k : k + 1], (8, 128)))
        shift = jnp.where(half, jnp.where(sub < 4, found[2], found[3]), jnp.where(sub < 4, found[0], found[1]))
        value = value + shift
        value = value - jnp.floor(value)
        weights.append(0.5 - jnp.abs(2.0 * value - 1.0))

    def row(a, i, k):
        return jnp.broadcast_to(rows[a, i, pl.ds(k, 1), :], (8, 128))

    def conduct_at(k, _):
        for i in range(LINES):
            e = (weights[0] * row(2, i, k) + weights[1] * row(3, i, k)) + (weights[2] * row(4, i, k) + weights[3] * row(5, i, k))
            cond[k + 1, i] = row(1, i, k) * jnp.exp(e)
            field[k + 1, i] = row(0, i, k) + row(6, i, k)
        return 0

    lax.fori_loop(0, WIDE, conduct_at, 0, unroll=8)

    top = lane % 64 == 0
    bottom = lane % 64 == 63

    def coefs_at(k, _):
        c = [HALF_DT * cond[k + 1, i] for i in range(LINES)]
        down = jnp.where(bottom, 0.0, pltpu.roll(c[0], 127, 1))
        for i in range(LINES):
            horiz[k + 1, i] = c[i] + HALF_DT * cond[k + 2, i]
        for i in range(3):
            mid[k, i] = c[i] + c[i + 1]
        cross[k] = jnp.where(bottom, 0.0, c[3] + down)
        ends[k, 0] = jnp.where(top, 1.0 - c[0], 1.0)
        ends[k, 1] = jnp.where(bottom, 1.0 - c[3], 1.0)
        return 0

    lax.fori_loop(0, WIDE, coefs_at, 0, unroll=8)

    def load(k):
        return tuple(field[k + 1, i] for i in range(LINES))

    def flux(k, u, right):
        return tuple(horiz[k + 1, i] * (right[i] - u[i]) for i in range(LINES))

    def sweep(first, last, source, save):
        low, count = first, WIDE - 2 * first
        blocks = -(-count // BLOCK)
        size = -(-count // blocks)

        def body(block, carry):
            before, u = carry
            base = low + block * size
            for n in range(size):
                k = base + n
                right = load(k + 1)
                after = flux(k, u, right)
                down = [mid[k, i] * (u[i + 1] - u[i]) for i in range(3)]
                down.append(cross[k] * (pltpu.roll(u[0], 127, 1) - u[3]))
                wrapped = pltpu.roll(down[3], 1, 1)
                for i in range(LINES):
                    y = (after[i] - before[i]) + (u[i] if 0 < i < 3 else ends[k, i // 3] * u[i])
                    if source is not None:
                        y = y + source(k, i)
                    y = (y + down[i]) - (down[i - 1] if i else wrapped)
                    field[k + 1, i] = y
                    if save:
                        extra[k, i] = y
                before, u = after, right
            return before, u

        u = load(low)
        lax.fori_loop(0, blocks, body, (flux(low - 1, load(low - 1), u), u))

        @pl.when(strip == 0)
        def _():
            for i in range(LINES):
                field[HALO, i] = zero

        @pl.when(strip == 127)
        def _():
            for i in range(LINES):
                field[WIDE - HALO + 1, i] = zero

    def steps(first, last, source, save=False):
        while first <= last:
            until = min(last, first + 3)

            def one(_, c, first=first):
                sweep(first, first, source, save)
                return c

            lax.fori_loop(0, until - first + 1, one, 0)
            first = until + 1

    control = lambda k, i: row(6, i, k)
    target = lambda k, i: row(7, i, k)
    misfit = lambda k, i: extra[k, i]

    steps(1, 15, control)
    steps(16, 16, target, True)

    def add_loss(k, total):
        return tuple(total[i] + extra[k, i] * extra[k, i] for i in range(LINES))

    loss = lax.fori_loop(HALO, HALO + CORE, add_loss, (zero,) * LINES, unroll=8)
    loss = jnp.sum((loss[0] + loss[1]) + (loss[2] + loss[3]), axis=(0, 1), keepdims=True)
    last = 16
    for power in (8, 4, 2, 1):
        steps(last + 1, last + power - 1, None)
        last += power
        steps(last, last, misfit, power > 1)
    steps(32, 32, None)

    inner = flat[6, :, HALO : HALO + CORE]
    squares = 0.5 * jnp.sum(inner * inner, axis=(0, 1), keepdims=True)
    wide_lane = lax.broadcasted_iota(jnp.int32, (256, CORE), 1)
    part[:, CORE:] = jnp.where(wide_lane == 0, loss, jnp.where(wide_lane == 1, squares, 0.0))
    part[:, :CORE] = 0.25 * inner
    for i in range(LINES):
        total = jnp.sum(field[pl.ds(HALO + 1, CORE), i], axis=1)
        total = (total + pltpu.roll(total, 64, 1)) * (DT / 32)
        part[pl.ds(i, 64, stride=4), :] += jnp.concatenate([total.T[:64], jnp.zeros((64, CORE), jnp.float32)], axis=1)


def heat(gen, pts, own, other):
    smem = pl.BlockSpec(memory_space=pltpu.SMEM)
    vmem = pl.BlockSpec(memory_space=pltpu.VMEM)
    f32 = jnp.float32
    return pl.pallas_call(
        heat_kernel,
        out_shape=jax.ShapeDtypeStruct((256, 128), f32),
        in_specs=[smem, smem, vmem, vmem],
        out_specs=vmem,
        scratch_shapes=[
            pltpu.VMEM((8, 16, 2, 8, 128), f32),
            pltpu.VMEM((8, LINES, WIDE, 128), f32),
            pltpu.VMEM((WIDE + 2, LINES, 8, 128), f32),
            pltpu.VMEM((WIDE + 1, LINES, 8, 128), f32),
            pltpu.VMEM((WIDE, 2, 8, 128), f32),
            pltpu.VMEM((WIDE, 3, 8, 128), f32),
            pltpu.VMEM((WIDE, 8, 128), f32),
            pltpu.VMEM((WIDE + 2, LINES, 8, 128), f32),
            pltpu.VMEM((WIDE, LINES, 8, 128), f32),
        ],
        compiler_params=pltpu.CompilerParams(vmem_limit_bytes=48 * 2**20),
    )(gen, pts, own, other)


def pack_kernel(shifts, start, base, modes, control, target, pieces, window, vector_of, sems, sem):
    shift_copy = pltpu.make_async_copy(shifts, vector_of, sem)
    shift_copy.start()
    block = position()[0]
    column = pl.multiple_of(block * 1024, 1024)
    before = pl.multiple_of(jnp.maximum(column - 128, 0), 128)
    after = pl.multiple_of(jnp.minimum(column + 1024, 8192 - 128), 128)
    sources = ((start, 0), (base, 1), (control, 6), (target, 7)) + tuple((modes.at[m], 2 + m) for m in range(4))
    copies = []
    for n, (source, a) in enumerate(sources):
        for part, (begin, to, length) in enumerate(((before, 0, 128), (column, 128, 1024), (after, 1152, 128))):
            copy = pltpu.make_async_copy(source.at[:, pl.ds(begin, length)], window.at[a, :, pl.ds(to, length)], sems.at[n, part])
            copy.start()
            copies.append(copy)
    for copy in copies:
        copy.wait()
    shift_copy.wait()

    @pl.when(block == 0)
    def _():
        window[:, :, :128] = jnp.zeros((8, 8, 128), jnp.float32)

    @pl.when(block == 7)
    def _():
        window[:, :, 1152:] = jnp.zeros((8, 8, 128), jnp.float32)

    lane = lax.broadcasted_iota(jnp.int32, (8, 128), 1)
    vector = jnp.zeros((8, 128), jnp.float32)
    for m in range(4):
        vector = jnp.where(lane == m, vector_of[0, m], vector)
    for a in range(8):
        for q in range(16):
            piece = window[a, :, 96 + 64 * q : 224 + 64 * q]
            pieces[q, a] = jnp.where(lane < 4, vector, piece) if a == 7 else piece


def pack(shifts, start, base, modes, control, target):
    hbm = pl.BlockSpec(memory_space=pltpu.HBM)
    return pl.pallas_call(
        pack_kernel,
        out_shape=jax.ShapeDtypeStruct((16, 8, 8, 128), jnp.float32),
        in_specs=[hbm] * 6,
        out_specs=pl.BlockSpec(memory_space=pltpu.VMEM),
        scratch_shapes=[pltpu.VMEM((8, 8, 1280), jnp.float32), pltpu.SMEM((1, 4), jnp.float32), pltpu.SemaphoreType.DMA((8, 3)), pltpu.SemaphoreType.DMA],
        compiler_params=pltpu.CompilerParams(vmem_limit_bytes=60 * 2**20),
    )(shifts, start, base, modes, control, target)


def spread_kernel(own, other, pieces, total):
    core = position()[2]
    total[...] = own[...] + other[...]
    lane = lax.broadcasted_iota(jnp.int32, (256, 128), 1)
    gradient = jnp.where(lane < CORE, total[...], 0.0)
    squares = jnp.sum(gradient * gradient, axis=(0, 1), keepdims=True)
    stats = pltpu.roll(total[:1], 64, 1)
    stats = jnp.where(lane[:1] < 2, stats, jnp.where(lane[:1] == 2, squares, 0.0))
    left = lane[:4] < CORE
    for q in range(16):
        rows = total[pl.ds(pl.multiple_of(16 * q + 8 * core, 8), 8), :]
        packed = jnp.where(left, rows[:4], pltpu.roll(rows[4:], 64, 1))
        for b in range(8):
            pieces[pl.ds(PIECE * (16 * b + q), 4), :] = packed
            pieces[pl.ds(PIECE * (16 * b + q) + 4, 1), :] = stats


def spread(own, other):
    vmem = pl.BlockSpec(memory_space=pltpu.VMEM)
    return pl.pallas_call(
        spread_kernel,
        out_shape=jax.ShapeDtypeStruct((128 * PIECE, 128), jnp.float32),
        in_specs=[vmem, vmem],
        out_specs=vmem,
        scratch_shapes=[pltpu.VMEM((256, 128), jnp.float32)],
        compiler_params=pltpu.CompilerParams(vmem_limit_bytes=8 * 2**20),
    )(own, other)


def finish_kernel(pieces, control, updated, objective):
    sums = [pieces[pl.ds(4 + i, 32, stride=4 * PIECE), :] for i in range(0, 4 * PIECE, PIECE)]
    stats = jnp.sum((sums[0] + sums[1]) + (sums[2] + sums[3]), axis=0, keepdims=True)
    lane = lax.broadcasted_iota(jnp.int32, (1, 128), 1)

    def entry(n):
        return jnp.sum(jnp.where(lane == n, stats, 0.0), axis=(0, 1), keepdims=True)

    cells = 256 * 8192
    objective[...] = (entry(0) * (0.5 / 32) + entry(1) * 0.25) / cells
    scaling = jnp.broadcast_to(0.5 / jnp.sqrt(entry(2) / cells + 1e-06), (4, 128))
    left = lax.broadcasted_iota(jnp.int32, (4, 128), 1) < CORE
    for n in range(64):
        columns = slice(128 * n, 128 * (n + 1))
        one, two = (pieces[pl.ds(PIECE * (2 * n + i), 4), :] for i in range(2))
        updated[:4, columns] = control[:4, columns] - scaling * jnp.where(left, one, pltpu.roll(two, 64, 1))
        updated[4:, columns] = control[4:, columns] - scaling * jnp.where(left, pltpu.roll(one, 64, 1), two)


def finish(pieces, control):
    vmem = pl.BlockSpec(memory_space=pltpu.VMEM)
    return pl.pallas_call(
        finish_kernel,
        out_shape=(jax.ShapeDtypeStruct((8, 8192), jnp.float32), jax.ShapeDtypeStruct((1, 1), jnp.float32)),
        in_specs=[vmem, vmem],
        out_specs=(vmem, vmem),
        compiler_params=pltpu.CompilerParams(vmem_limit_bytes=8 * 2**20),
    )(pieces, control)


def local(start_state, base_field, modes, control, target, shifts, gen_vector, point_ids):
    sent = pack(shifts, start_state, base_field, modes, control, target)
    own = lax.all_to_all(sent, LINKS, 0, 0, axis_index_groups=BLOCK_GROUPS, tiled=True)
    other = lax.ppermute(own, "slab", PAIRS)
    part = heat(gen_vector, point_ids, own, other)
    pieces = spread(part, lax.ppermute(part, "slab", PAIRS))
    pieces = pieces.reshape(128, 1, PIECE * 128)
    pieces = lax.all_to_all(pieces, LINKS, 0, 0, axis_index_groups=CORE_GROUPS, tiled=True)
    pieces = pieces.reshape(128 * PIECE, 128)
    new_control, objective = finish(pieces, control)
    return new_control, objective[0, 0]


def solution(mesh):
    return jax.shard_map(
        local,
        mesh=mesh,
        in_specs=(
            P("slab", None),
            P("slab", None),
            P(None, "slab", None),
            P("slab", None),
            P("slab", None),
            P("shift", None),
            P(),
            P(),
        ),
        out_specs=(P("slab", None), P()),
        check_vma=False,
    )
```

```python
import jax
import jax.numpy as jnp
from jax import lax
from jax.experimental import pallas as pl
from jax.experimental.pallas import tpu as pltpu
from jax.sharding import PartitionSpec as P

NLAT = 1021
HALF_DT = 0.02
DT = 0.04
HALO = 32
WIDE = 128
CORE = 64
LINES = 4
BLOCK = 43
PIECE = 5
LINKS = ("shift", "slab")


X_OFF = (2, 1, 0, 1, 3, 2, 3, 0, 3, 0, 3, 2, 0, 1, 2, 1)
X_BITS = sum(x << (2 * q) for q, x in enumerate(X_OFF[:8])), sum(x << (2 * q) for q, x in enumerate(X_OFF[8:]))
SHIFT_ROWS = tuple(tuple(16 * (8 * c + X_OFF[8 * c : 8 * c + 8].index(x)) for x in range(4)) for c in range(2))


def position():
    shift, slab = lax.axis_index("shift"), lax.axis_index("slab")
    z_low, y, core = lax.div(slab, 8), lax.rem(lax.div(slab, 2), 4), lax.rem(slab, 2)
    z_high, x = lax.div(shift, 4), lax.rem(shift, 4)
    place = z_low * 4 + y
    bits = jnp.where(place < 8, X_BITS[0], X_BITS[1])
    offset = lax.rem(lax.shift_right_logical(bits, 2 * lax.rem(place, 8)), 4)
    block = lax.rem(z_high + 1 - lax.div(z_low, 2), 2) * 4 + lax.rem(x - offset + 4, 4)
    return block, place, core


def device_at(block, place, core):
    z_low, y = divmod(place, 4)
    z_high, x = divmod(block, 4)
    return ((z_high ^ (1 - z_low // 2)) * 4 + (x + X_OFF[place]) % 4) * 32 + z_low * 8 + y * 2 + core


BLOCK_GROUPS = [[device_at(b, q, c) for q in range(16)] for b in range(8) for c in range(2)]
CORE_GROUPS = [[device_at(b, q, c) for b in range(8) for q in range(16)] for c in range(2)]
PAIRS = [(i, i ^ 1) for i in range(32)]


def heat_kernel(gen, pts, own, other, part, tall, rows, horiz, ends, mid, cross, field, extra):
    lane = lax.broadcasted_iota(jnp.int32, (8, 128), 1)
    sub = lax.broadcasted_iota(jnp.int32, (8, 128), 0)
    half = lane >= 64
    block, place, core = position()
    strip = block * 16 + place

    for a in range(8):
        for q in range(16):
            tall[a, q, core] = own[q, a]
            tall[a, q, 1 - core] = other[q, a]
    flat = tall.reshape(8, 256, 128)
    zero = jnp.zeros((8, 128), jnp.float32)
    for i in range(LINES):
        field[0, i] = zero
        field[WIDE + 1, i] = zero
        horiz[WIDE, i] = zero

    scales = {1: HALF_DT, 6: DT, 7: -1.0}
    first_half = lax.broadcasted_iota(jnp.int32, (WIDE, 128), 1) < 64
    for a in (1, 2, 3, 4, 5, 6, 0, 7):
        for i in range(0, LINES, 2):
            pair = [flat[a, pl.ds(i + n, 64, stride=4), :] for n in range(2)]
            turned = jnp.concatenate(pair, axis=0).T
            if a in scales:
                turned = scales[a] * turned
            swapped = pltpu.roll(turned, 64, 1)
            rows[a, i] = jnp.where(first_half, turned, swapped)
            rows[a, i + 1] = jnp.where(first_half, swapped, turned)
            if a == 0:
                for n in range(2):
                    rows[a, i + n] += rows[6, i + n]

    weights = []
    for k in range(4):
        product = [lax.rem(pts[p] * gen[k], NLAT).astype(jnp.float32) / NLAT for p in range(4)]
        value = jnp.where(sub % 4 == 0, product[0], jnp.where(sub % 4 == 1, product[1], jnp.where(sub % 4 == 2, product[2], product[3])))
        found = []
        for y in range(4):
            line = flat[7, pl.ds(jnp.where(core == 0, SHIFT_ROWS[0][y], SHIFT_ROWS[1][y]), 1), :]
            found.append(jnp.broadcast_to(line[:, k : k + 1], (8, 128)))
        shift = jnp.where(half, jnp.where(sub < 4, found[2], found[3]), jnp.where(sub < 4, found[0], found[1]))
        value = value + shift
        value = value - jnp.floor(value)
        weights.append(0.5 - jnp.abs(2.0 * value - 1.0))

    def row(a, i, k):
        return jnp.broadcast_to(rows[a, i, pl.ds(k, 1), :], (8, 128))

    top = lane % 64 == 0
    bottom = lane % 64 == 63

    def coefs_at(k, left):
        c = []
        for i in range(LINES):
            e = (weights[0] * row(2, i, k) + weights[1] * row(3, i, k)) + (weights[2] * row(4, i, k) + weights[3] * row(5, i, k))
            c.append(row(1, i, k) * jnp.exp(e))
            horiz[k, i] = left[i] + c[i]
            field[k + 1, i] = row(0, i, k)
        for i in range(3):
            mid[k, i] = c[i] + c[i + 1]
        cross[k] = jnp.where(bottom, 0.0, c[3] + pltpu.roll(c[0], 127, 1))
        ends[k, 0] = jnp.where(top, 1.0 - c[0], 1.0)
        ends[k, 1] = jnp.where(bottom, 1.0 - c[3], 1.0)
        return tuple(c)

    lax.fori_loop(0, WIDE, coefs_at, (zero,) * LINES, unroll=16)

    def load(k):
        return tuple(field[k + 1, i] for i in range(LINES))

    def flux(k, u, right):
        return tuple(horiz[k + 1, i] * (right[i] - u[i]) for i in range(LINES))

    def sweep(first, last, source, save):
        low, count = first, WIDE - 2 * first
        blocks = -(-count // BLOCK)
        size = -(-count // blocks)

        def body(block, carry):
            before, u = carry
            base = low + block * size
            for n in range(size):
                k = base + n
                right = load(k + 1)
                after = flux(k, u, right)
                down = [mid[k, i] * (u[i + 1] - u[i]) for i in range(3)]
                down.append(cross[k] * (pltpu.roll(u[0], 127, 1) - u[3]))
                wrapped = pltpu.roll(down[3], 1, 1)
                for i in range(LINES):
                    y = (after[i] - before[i]) + (u[i] if 0 < i < 3 else ends[k, i // 3] * u[i])
                    if source is not None:
                        y = y + source(k, i)
                    y = (y + down[i]) - (down[i - 1] if i else wrapped)
                    field[k + 1, i] = y
                    if save:
                        extra[k, i] = y
                before, u = after, right
            return before, u

        u = load(low)
        lax.fori_loop(0, blocks, body, (flux(low - 1, load(low - 1), u), u))

        @pl.when(strip == 0)
        def _():
            for i in range(LINES):
                field[HALO, i] = zero

        @pl.when(strip == 127)
        def _():
            for i in range(LINES):
                field[WIDE - HALO + 1, i] = zero

    def steps(first, last, source, save=False):
        while first <= last:
            until = min(last, first + 3)

            def one(_, c, first=first):
                sweep(first, first, source, save)
                return c

            lax.fori_loop(0, until - first + 1, one, 0)
            first = until + 1

    control = lambda k, i: row(6, i, k)
    target = lambda k, i: row(7, i, k)
    misfit = lambda k, i: extra[k, i]

    steps(1, 15, control)
    steps(16, 16, target, True)

    def add_loss(k, total):
        return tuple(total[i] + extra[k, i] * extra[k, i] for i in range(LINES))

    loss = lax.fori_loop(HALO, HALO + CORE, add_loss, (zero,) * LINES, unroll=8)
    loss = jnp.sum((loss[0] + loss[1]) + (loss[2] + loss[3]), axis=(0, 1), keepdims=True)
    last = 16
    for power in (8, 4, 2, 1):
        steps(last + 1, last + power - 1, None)
        last += power
        steps(last, last, misfit, power > 1)
    steps(32, 32, None)

    inner = flat[6, :, HALO : HALO + CORE]
    squares = 0.5 * jnp.sum(inner * inner, axis=(0, 1), keepdims=True)
    wide_lane = lax.broadcasted_iota(jnp.int32, (256, CORE), 1)
    part[:, CORE:] = jnp.where(wide_lane == 0, loss, jnp.where(wide_lane == 1, squares, 0.0))
    part[:, :CORE] = 0.25 * inner
    for i in range(LINES):
        total = jnp.sum(field[pl.ds(HALO + 1, CORE), i], axis=1)
        total = (total + pltpu.roll(total, 64, 1)) * (DT / 32)
        part[pl.ds(i, 64, stride=4), :] += jnp.concatenate([total.T[:64], jnp.zeros((64, CORE), jnp.float32)], axis=1)


def heat(gen, pts, own, other):
    smem = pl.BlockSpec(memory_space=pltpu.SMEM)
    vmem = pl.BlockSpec(memory_space=pltpu.VMEM)
    f32 = jnp.float32
    return pl.pallas_call(
        heat_kernel,
        out_shape=jax.ShapeDtypeStruct((256, 128), f32),
        in_specs=[smem, smem, vmem, vmem],
        out_specs=vmem,
        scratch_shapes=[
            pltpu.VMEM((8, 16, 2, 8, 128), f32),
            pltpu.VMEM((8, LINES, WIDE, 128), f32),
            pltpu.VMEM((WIDE + 1, LINES, 8, 128), f32),
            pltpu.VMEM((WIDE, 2, 8, 128), f32),
            pltpu.VMEM((WIDE, 3, 8, 128), f32),
            pltpu.VMEM((WIDE, 8, 128), f32),
            pltpu.VMEM((WIDE + 2, LINES, 8, 128), f32),
            pltpu.VMEM((WIDE, LINES, 8, 128), f32),
        ],
        compiler_params=pltpu.CompilerParams(vmem_limit_bytes=48 * 2**20),
    )(gen, pts, own, other)


def pack_kernel(shifts, start, base, modes, control, target, pieces, window, packed, vector_of, sems, out_sems, shift_sem):
    block = position()[0]
    shift_copy = pltpu.make_async_copy(shifts, vector_of, shift_sem)
    shift_copy.start()
    column = pl.multiple_of(block * 1024, 1024)
    before = pl.multiple_of(jnp.maximum(column - 128, 0), 128)
    after = pl.multiple_of(jnp.minimum(column + 1024, 8192 - 128), 128)
    sources = ((start, 0), (base, 1), (control, 6), (target, 7), (modes, slice(2, 6)))
    copies = []
    for n, (source, a) in enumerate(sources):
        group = []
        for part, (begin, to, length) in enumerate(((before, 0, 128), (column, 128, 1024), (after, 1152, 128))):
            group.append(
                pltpu.make_async_copy(
                    source.at[..., pl.ds(begin, length)], window.at[a, :, pl.ds(to, length)], sems.at[n, part]
                )
            )
            group[-1].start()
        copies.append(group)
    shift_copy.wait()
    lane = lax.broadcasted_iota(jnp.int32, (8, 128), 1)
    vector = jnp.zeros((8, 128), jnp.float32)
    for m in range(4):
        vector = jnp.where(lane == m, vector_of[0, m], vector)
    inside = {
        0: jnp.logical_or(lane >= HALO, block > 0),
        15: jnp.logical_or(lane < WIDE - HALO, block < 7),
    }
    sends = []
    for group, arrays in zip(copies, ((0,), (1,), (6,), (7,), (2, 3, 4, 5))):
        for copy in group:
            copy.wait()
        for a in arrays:
            for q in range(16):
                piece = window[a, :, 96 + 64 * q : 224 + 64 * q]
                if q in inside:
                    piece = jnp.where(inside[q], piece, 0.0)
                if a == 7:
                    piece = jnp.where(lane < 4, vector, piece)
                packed[a, q] = piece
            sends.append(pltpu.make_async_copy(packed.at[a], pieces.at[:, a], out_sems.at[a]))
            sends[-1].start()
    for send in sends:
        send.wait()


def pack(shifts, start, base, modes, control, target):
    hbm = pl.BlockSpec(memory_space=pltpu.HBM)
    f32 = jnp.float32
    return pl.pallas_call(
        pack_kernel,
        out_shape=jax.ShapeDtypeStruct((16, 8, 8, 128), f32),
        in_specs=[hbm] * 6,
        out_specs=hbm,
        scratch_shapes=[
            pltpu.VMEM((8, 8, 1280), f32),
            pltpu.VMEM((8, 16, 8, 128), f32),
            pltpu.SMEM((1, 4), f32),
            pltpu.SemaphoreType.DMA((5, 3)),
            pltpu.SemaphoreType.DMA((8,)),
            pltpu.SemaphoreType.DMA,
        ],
        compiler_params=pltpu.CompilerParams(vmem_limit_bytes=60 * 2**20),
    )(shifts, start, base, modes, control, target)


def spread_kernel(own, other, pieces, total):
    core = position()[2]
    total[...] = own[...] + other[...]
    lane = lax.broadcasted_iota(jnp.int32, (256, 128), 1)
    gradient = jnp.where(lane < CORE, total[...], 0.0)
    squares = jnp.sum(gradient * gradient, axis=(0, 1), keepdims=True)
    stats = pltpu.roll(total[:1], 64, 1)
    stats = jnp.where(lane[:1] < 2, stats, jnp.where(lane[:1] == 2, squares, 0.0))
    left = lane[:4] < CORE
    for q in range(16):
        rows = total[pl.ds(pl.multiple_of(16 * q + 8 * core, 8), 8), :]
        packed = jnp.where(left, rows[:4], pltpu.roll(rows[4:], 64, 1))
        for b in range(8):
            pieces[pl.ds(PIECE * (16 * b + q), 4), :] = packed
            pieces[pl.ds(PIECE * (16 * b + q) + 4, 1), :] = stats


def spread(own, other):
    vmem = pl.BlockSpec(memory_space=pltpu.VMEM)
    return pl.pallas_call(
        spread_kernel,
        out_shape=jax.ShapeDtypeStruct((128 * PIECE, 128), jnp.float32),
        in_specs=[vmem, vmem],
        out_specs=vmem,
        scratch_shapes=[pltpu.VMEM((256, 128), jnp.float32)],
        compiler_params=pltpu.CompilerParams(vmem_limit_bytes=8 * 2**20),
    )(own, other)


def finish_kernel(pieces, control, updated, objective):
    sums = [pieces[pl.ds(4 + i, 32, stride=4 * PIECE), :] for i in range(0, 4 * PIECE, PIECE)]
    stats = jnp.sum((sums[0] + sums[1]) + (sums[2] + sums[3]), axis=0, keepdims=True)
    lane = lax.broadcasted_iota(jnp.int32, (1, 128), 1)

    def entry(n):
        return jnp.sum(jnp.where(lane == n, stats, 0.0), axis=(0, 1), keepdims=True)

    cells = 256 * 8192
    objective[...] = (entry(0) * (0.5 / 32) + entry(1) * 0.25) / cells
    scaling = jnp.broadcast_to(0.5 / jnp.sqrt(entry(2) / cells + 1e-06), (4, 128))
    left = lax.broadcasted_iota(jnp.int32, (4, 128), 1) < CORE
    for n in range(64):
        columns = slice(128 * n, 128 * (n + 1))
        one, two = (pieces[pl.ds(PIECE * (2 * n + i), 4), :] for i in range(2))
        updated[:4, columns] = control[:4, columns] - scaling * jnp.where(left, one, pltpu.roll(two, 64, 1))
        updated[4:, columns] = control[4:, columns] - scaling * jnp.where(left, pltpu.roll(one, 64, 1), two)


def finish(pieces, control):
    vmem = pl.BlockSpec(memory_space=pltpu.VMEM)
    return pl.pallas_call(
        finish_kernel,
        out_shape=(jax.ShapeDtypeStruct((8, 8192), jnp.float32), jax.ShapeDtypeStruct((1, 1), jnp.float32)),
        in_specs=[vmem, vmem],
        out_specs=(vmem, vmem),
        compiler_params=pltpu.CompilerParams(vmem_limit_bytes=8 * 2**20),
    )(pieces, control)


def local(start_state, base_field, modes, control, target, shifts, gen_vector, point_ids):
    sent = pack(shifts, start_state, base_field, modes, control, target)
    own = lax.all_to_all(sent, LINKS, 0, 0, axis_index_groups=BLOCK_GROUPS, tiled=True)
    other = lax.ppermute(own, "slab", PAIRS)
    part = heat(gen_vector, point_ids, own, other)
    pieces = spread(part, lax.ppermute(part, "slab", PAIRS))
    pieces = pieces.reshape(128, 1, PIECE * 128)
    pieces = lax.all_to_all(pieces, LINKS, 0, 0, axis_index_groups=CORE_GROUPS, tiled=True)
    pieces = pieces.reshape(128 * PIECE, 128)
    new_control, objective = finish(pieces, control)
    return new_control, objective[0, 0]


def solution(mesh):
    return jax.shard_map(
        local,
        mesh=mesh,
        in_specs=(
            P("slab", None),
            P("slab", None),
            P(None, "slab", None),
            P("slab", None),
            P("slab", None),
            P("shift", None),
            P(),
            P(),
        ),
        out_specs=(P("slab", None), P()),
        check_vma=False,
    )
```

```python
import jax
import jax.numpy as jnp
from jax import lax
from jax.experimental import pallas as pl
from jax.experimental.pallas import tpu as pltpu
from jax.sharding import PartitionSpec as P

NLAT = 1021
HALF_DT = 0.02
DT = 0.04
HALO = 32
WIDE = 128
CORE = 64
LINES = 4
BLOCK = 43
PIECE = 5
LINKS = ("shift", "slab")


def position():
    slab = lax.axis_index("slab")
    return lax.axis_index("shift"), lax.div(slab, 2), lax.rem(slab, 2)


def device_at(z_high, x, place, core):
    return (z_high * 4 + x % 4) * 32 + place * 2 + core


BLOCK_GROUPS = [[device_at(h, x, q, c) for q in range(16)] for h in range(2) for x in range(4) for c in range(2)]
AHEAD = (2, 1, 0, 1, 3, 2, 3, 0, 3, 0, 3, 2, 0, 1, 2, 1)
ORDER = [((h + 1 - q // 8) % 2, (x + AHEAD[q]) % 4, q) for h in range(2) for x in range(4) for q in range(16)]
PLACES = [ORDER.index((h, x, q)) for h in range(2) for x in range(4) for q in range(16)]
CORE_GROUPS = [[device_at(*member, c) for member in ORDER] for c in range(2)]
PAIRS = [(i, i ^ 1) for i in range(32)]
SHIFT_MOVES = [
    [
        (device_at(h, x + step, q, c), device_at(h ^ c, x, q, c))
        for h in range(2)
        for x in range(4)
        for q in range(16)
        for c in range(2)
    ]
    for step in range(4)
]


def heat_kernel(gen, pts, shift0, shift1, shift2, shift3, own, other, part, tall, rows, horiz, ends, mid, cross, field, extra):
    lane = lax.broadcasted_iota(jnp.int32, (8, 128), 1)
    sub = lax.broadcasted_iota(jnp.int32, (8, 128), 0)
    half = lane >= 64
    block, place, core = position()
    strip = block * 16 + place

    for a in range(8):
        for q in range(16):
            tall[a, q, core] = own[q, a]
            tall[a, q, 1 - core] = other[q, a]
    flat = tall.reshape(8, 256, 128)
    zero = jnp.zeros((8, 128), jnp.float32)
    for i in range(LINES):
        field[0, i] = zero
        field[WIDE + 1, i] = zero
        horiz[WIDE, i] = zero

    scales = {1: HALF_DT, 6: DT, 7: -1.0}
    first_half = lax.broadcasted_iota(jnp.int32, (WIDE, 128), 1) < 64
    for a in (1, 2, 3, 4, 5, 6, 0, 7):
        for i in range(0, LINES, 2):
            pair = [flat[a, pl.ds(i + n, 64, stride=4), :] for n in range(2)]
            turned = jnp.concatenate(pair, axis=0).T
            if a in scales:
                turned = scales[a] * turned
            swapped = pltpu.roll(turned, 64, 1)
            rows[a, i] = jnp.where(first_half, turned, swapped)
            rows[a, i + 1] = jnp.where(first_half, swapped, turned)
            if a == 0:
                for n in range(2):
                    rows[a, i + n] += rows[6, i + n]

    weights = []
    for k in range(4):
        product = [lax.rem(pts[p] * gen[k], NLAT).astype(jnp.float32) / NLAT for p in range(4)]
        value = jnp.where(sub % 4 == 0, product[0], jnp.where(sub % 4 == 1, product[1], jnp.where(sub % 4 == 2, product[2], product[3])))
        found = [jnp.broadcast_to(vector[...][:, k : k + 1], (8, 128)) for vector in (shift0, shift1, shift2, shift3)]
        shift = jnp.where(half, jnp.where(sub < 4, found[2], found[3]), jnp.where(sub < 4, found[0], found[1]))
        value = value + shift
        value = value - jnp.floor(value)
        weights.append(0.5 - jnp.abs(2.0 * value - 1.0))

    def row(a, i, k):
        return jnp.broadcast_to(rows[a, i, pl.ds(k, 1), :], (8, 128))

    top = lane % 64 == 0
    bottom = lane % 64 == 63

    def coefs_at(k, left):
        c = []
        for i in range(LINES):
            e = (weights[0] * row(2, i, k) + weights[1] * row(3, i, k)) + (weights[2] * row(4, i, k) + weights[3] * row(5, i, k))
            c.append(row(1, i, k) * jnp.exp(e))
            horiz[k, i] = left[i] + c[i]
            field[k + 1, i] = row(0, i, k)
        for i in range(3):
            mid[k, i] = c[i] + c[i + 1]
        cross[k] = jnp.where(bottom, 0.0, c[3] + pltpu.roll(c[0], 127, 1))
        ends[k, 0] = jnp.where(top, 1.0 - c[0], 1.0)
        ends[k, 1] = jnp.where(bottom, 1.0 - c[3], 1.0)
        return tuple(c)

    lax.fori_loop(0, WIDE, coefs_at, (zero,) * LINES, unroll=16)

    def load(k):
        return tuple(field[k + 1, i] for i in range(LINES))

    def flux(k, u, right):
        return tuple(horiz[k + 1, i] * (right[i] - u[i]) for i in range(LINES))

    def sweep(first, last, source, save):
        low, count = first, WIDE - 2 * first
        blocks = -(-count // BLOCK)
        size = -(-count // blocks)

        def body(block, carry):
            before, u = carry
            base = low + block * size
            for n in range(size):
                k = base + n
                right = load(k + 1)
                after = flux(k, u, right)
                down = [mid[k, i] * (u[i + 1] - u[i]) for i in range(3)]
                down.append(cross[k] * (pltpu.roll(u[0], 127, 1) - u[3]))
                wrapped = pltpu.roll(down[3], 1, 1)
                for i in range(LINES):
                    y = (after[i] - before[i]) + (u[i] if 0 < i < 3 else ends[k, i // 3] * u[i])
                    if source is not None:
                        y = y + source(k, i)
                    y = (y + down[i]) - (down[i - 1] if i else wrapped)
                    field[k + 1, i] = y
                    if save:
                        extra[k, i] = y
                before, u = after, right
            return before, u

        u = load(low)
        lax.fori_loop(0, blocks, body, (flux(low - 1, load(low - 1), u), u))

        @pl.when(strip == 0)
        def _():
            for i in range(LINES):
                field[HALO, i] = zero

        @pl.when(strip == 127)
        def _():
            for i in range(LINES):
                field[WIDE - HALO + 1, i] = zero

    def steps(first, last, source, save=False):
        while first <= last:
            until = min(last, first + 3)

            def one(_, c, first=first):
                sweep(first, first, source, save)
                return c

            lax.fori_loop(0, until - first + 1, one, 0)
            first = until + 1

    control = lambda k, i: row(6, i, k)
    target = lambda k, i: row(7, i, k)
    misfit = lambda k, i: extra[k, i]

    steps(1, 15, control)
    steps(16, 16, target, True)

    def add_loss(k, total):
        return tuple(total[i] + extra[k, i] * extra[k, i] for i in range(LINES))

    loss = lax.fori_loop(HALO, HALO + CORE, add_loss, (zero,) * LINES, unroll=8)
    loss = jnp.sum((loss[0] + loss[1]) + (loss[2] + loss[3]), axis=(0, 1), keepdims=True)
    last = 16
    for power in (8, 4, 2, 1):
        steps(last + 1, last + power - 1, None)
        last += power
        steps(last, last, misfit, power > 1)
    steps(32, 32, None)

    inner = flat[6, :, HALO : HALO + CORE]
    squares = 0.5 * jnp.sum(inner * inner, axis=(0, 1), keepdims=True)
    wide_lane = lax.broadcasted_iota(jnp.int32, (256, CORE), 1)
    part[:, CORE:] = jnp.where(wide_lane == 0, loss, jnp.where(wide_lane == 1, squares, 0.0))
    part[:, :CORE] = 0.25 * inner
    for i in range(LINES):
        total = jnp.sum(field[pl.ds(HALO + 1, CORE), i], axis=1)
        total = (total + pltpu.roll(total, 64, 1)) * (DT / 32)
        part[pl.ds(i, 64, stride=4), :] += jnp.concatenate([total.T[:64], jnp.zeros((64, CORE), jnp.float32)], axis=1)


def heat(gen, pts, vectors, own, other):
    smem = pl.BlockSpec(memory_space=pltpu.SMEM)
    vmem = pl.BlockSpec(memory_space=pltpu.VMEM)
    f32 = jnp.float32
    return pl.pallas_call(
        heat_kernel,
        out_shape=jax.ShapeDtypeStruct((256, 128), f32),
        in_specs=[smem, smem] + [vmem] * 6,
        out_specs=vmem,
        scratch_shapes=[
            pltpu.VMEM((8, 16, 2, 8, 128), f32),
            pltpu.VMEM((8, LINES, WIDE, 128), f32),
            pltpu.VMEM((WIDE + 1, LINES, 8, 128), f32),
            pltpu.VMEM((WIDE, 2, 8, 128), f32),
            pltpu.VMEM((WIDE, 3, 8, 128), f32),
            pltpu.VMEM((WIDE, 8, 128), f32),
            pltpu.VMEM((WIDE + 2, LINES, 8, 128), f32),
            pltpu.VMEM((WIDE, LINES, 8, 128), f32),
        ],
        compiler_params=pltpu.CompilerParams(vmem_limit_bytes=48 * 2**20),
    )(gen, pts, *vectors, own, other)


def pack_kernel(start, base, modes, control, target, pieces, window, packed, sems, out_sems):
    block = position()[0]
    column = pl.multiple_of(block * 1024, 1024)
    before = pl.multiple_of(jnp.maximum(column - 128, 0), 128)
    after = pl.multiple_of(jnp.minimum(column + 1024, 8192 - 128), 128)
    sources = ((start, 0), (base, 1), (control, 6), (target, 7), (modes, slice(2, 6)))
    copies = []
    for n, (source, a) in enumerate(sources):
        group = []
        for part, (begin, to, length) in enumerate(((before, 0, 128), (column, 128, 1024), (after, 1152, 128))):
            group.append(
                pltpu.make_async_copy(
                    source.at[..., pl.ds(begin, length)], window.at[a, :, pl.ds(to, length)], sems.at[n, part]
                )
            )
            group[-1].start()
        copies.append(group)
    lane = lax.broadcasted_iota(jnp.int32, (8, 128), 1)
    inside = {
        0: jnp.logical_or(lane >= HALO, block > 0),
        15: jnp.logical_or(lane < WIDE - HALO, block < 7),
    }
    sends = []
    for group, arrays in zip(copies, ((0,), (1,), (6,), (7,), (2, 3, 4, 5))):
        for copy in group:
            copy.wait()
        for a in arrays:
            for q in range(16):
                piece = window[a, :, 96 + 64 * q : 224 + 64 * q]
                if q in inside:
                    piece = jnp.where(inside[q], piece, 0.0)
                packed[a, q] = piece
            sends.append(pltpu.make_async_copy(packed.at[a], pieces.at[:, a], out_sems.at[a]))
            sends[-1].start()
    for send in sends:
        send.wait()


def pack(start, base, modes, control, target):
    hbm = pl.BlockSpec(memory_space=pltpu.HBM)
    f32 = jnp.float32
    return pl.pallas_call(
        pack_kernel,
        out_shape=jax.ShapeDtypeStruct((16, 8, 8, 128), f32),
        in_specs=[hbm] * 5,
        out_specs=hbm,
        scratch_shapes=[
            pltpu.VMEM((8, 8, 1280), f32),
            pltpu.VMEM((8, 16, 8, 128), f32),
            pltpu.SemaphoreType.DMA((5, 3)),
            pltpu.SemaphoreType.DMA((8,)),
        ],
        compiler_params=pltpu.CompilerParams(vmem_limit_bytes=60 * 2**20),
    )(start, base, modes, control, target)


def spread_kernel(own, other, pieces, total):
    core = position()[2]
    total[...] = own[...] + other[...]
    lane = lax.broadcasted_iota(jnp.int32, (256, 128), 1)
    gradient = jnp.where(lane < CORE, total[...], 0.0)
    squares = jnp.sum(gradient * gradient, axis=(0, 1), keepdims=True)
    stats = pltpu.roll(total[:1], 64, 1)
    stats = jnp.where(lane[:1] < 2, stats, jnp.where(lane[:1] == 2, squares, 0.0))
    left = lane[:4] < CORE
    for q in range(16):
        rows = total[pl.ds(pl.multiple_of(16 * q + 8 * core, 8), 8), :]
        packed = jnp.where(left, rows[:4], pltpu.roll(rows[4:], 64, 1))
        for n in range(q, 128, 16):
            pieces[pl.ds(PIECE * n, 4), :] = packed
            pieces[pl.ds(PIECE * n + 4, 1), :] = stats


def spread(own, other):
    vmem = pl.BlockSpec(memory_space=pltpu.VMEM)
    return pl.pallas_call(
        spread_kernel,
        out_shape=jax.ShapeDtypeStruct((128 * PIECE, 128), jnp.float32),
        in_specs=[vmem, vmem],
        out_specs=vmem,
        scratch_shapes=[pltpu.VMEM((256, 128), jnp.float32)],
        compiler_params=pltpu.CompilerParams(vmem_limit_bytes=8 * 2**20),
    )(own, other)


def finish_kernel(pieces, control, updated, objective):
    sums = [pieces[pl.ds(4 + i, 32, stride=4 * PIECE), :] for i in range(0, 4 * PIECE, PIECE)]
    stats = jnp.sum((sums[0] + sums[1]) + (sums[2] + sums[3]), axis=0, keepdims=True)
    lane = lax.broadcasted_iota(jnp.int32, (1, 128), 1)

    def entry(n):
        return jnp.sum(jnp.where(lane == n, stats, 0.0), axis=(0, 1), keepdims=True)

    cells = 256 * 8192
    objective[...] = (entry(0) * (0.5 / 32) + entry(1) * 0.25) / cells
    scaling = jnp.broadcast_to(0.5 / jnp.sqrt(entry(2) / cells + 1e-06), (4, 128))
    left = lax.broadcasted_iota(jnp.int32, (4, 128), 1) < CORE
    for n in range(64):
        columns = slice(128 * n, 128 * (n + 1))
        one, two = (pieces[pl.ds(PIECE * PLACES[2 * n + i], 4), :] for i in range(2))
        updated[:4, columns] = control[:4, columns] - scaling * jnp.where(left, one, pltpu.roll(two, 64, 1))
        updated[4:, columns] = control[4:, columns] - scaling * jnp.where(left, pltpu.roll(one, 64, 1), two)


def finish(pieces, control):
    vmem = pl.BlockSpec(memory_space=pltpu.VMEM)
    return pl.pallas_call(
        finish_kernel,
        out_shape=(jax.ShapeDtypeStruct((8, 8192), jnp.float32), jax.ShapeDtypeStruct((1, 1), jnp.float32)),
        in_specs=[vmem, vmem],
        out_specs=(vmem, vmem),
        compiler_params=pltpu.CompilerParams(vmem_limit_bytes=8 * 2**20),
    )(pieces, control)


def local(start_state, base_field, modes, control, target, shifts, gen_vector, point_ids):
    vectors = [lax.ppermute(shifts, LINKS, moves) for moves in SHIFT_MOVES]
    sent = pack(start_state, base_field, modes, control, target)
    own = lax.all_to_all(sent, LINKS, 0, 0, axis_index_groups=BLOCK_GROUPS, tiled=True)
    own, vectors = lax.optimization_barrier((own, vectors))
    other = lax.ppermute(own, "slab", PAIRS)
    part = heat(gen_vector, point_ids, vectors, own, other)
    pieces = spread(part, lax.ppermute(part, "slab", PAIRS))
    pieces = pieces.reshape(128, 1, PIECE * 128)
    pieces = lax.all_to_all(pieces, LINKS, 0, 0, axis_index_groups=CORE_GROUPS, tiled=True)
    pieces = pieces.reshape(128 * PIECE, 128)
    new_control, objective = finish(pieces, control)
    return new_control, objective[0, 0]


def solution(mesh):
    return jax.shard_map(
        local,
        mesh=mesh,
        in_specs=(
            P("slab", None),
            P("slab", None),
            P(None, "slab", None),
            P("slab", None),
            P("slab", None),
            P("shift", None),
            P(),
            P(),
        ),
        out_specs=(P("slab", None), P()),
        check_vma=False,
    )
```

```python
import jax
import jax.numpy as jnp
from jax import lax
from jax.experimental import pallas as pl
from jax.experimental.pallas import tpu as pltpu
from jax.sharding import PartitionSpec as P

NLAT = 1021
HALF_DT = 0.02
DT = 0.04
HALO = 32
WIDE = 128
CORE = 64
LINES = 4
GROUP = 4
PIECE = 5
LINKS = ("shift", "slab")


X_OFF = (2, 1, 0, 1, 3, 2, 3, 0, 3, 0, 3, 2, 0, 1, 2, 1)
X_BITS = sum(x << (2 * q) for q, x in enumerate(X_OFF[:8])), sum(x << (2 * q) for q, x in enumerate(X_OFF[8:]))
SHIFT_ROWS = tuple(tuple(16 * (8 * c + X_OFF[8 * c : 8 * c + 8].index(x)) for x in range(4)) for c in range(2))


def position():
    shift, slab = lax.axis_index("shift"), lax.axis_index("slab")
    z_low, y, core = lax.div(slab, 8), lax.rem(lax.div(slab, 2), 4), lax.rem(slab, 2)
    z_high, x = lax.div(shift, 4), lax.rem(shift, 4)
    place = z_low * 4 + y
    bits = jnp.where(place < 8, X_BITS[0], X_BITS[1])
    offset = lax.rem(lax.shift_right_logical(bits, 2 * lax.rem(place, 8)), 4)
    block = lax.rem(z_high + 1 - lax.div(z_low, 2), 2) * 4 + lax.rem(x - offset + 4, 4)
    return block, place, core


def device_at(block, place, core):
    z_low, y = divmod(place, 4)
    z_high, x = divmod(block, 4)
    return ((z_high ^ (1 - z_low // 2)) * 4 + (x + X_OFF[place]) % 4) * 32 + z_low * 8 + y * 2 + core


BLOCK_GROUPS = [[device_at(b, q, c) for q in range(16)] for b in range(8) for c in range(2)]
CORE_GROUPS = [[device_at(b, q, c) for b in range(8) for q in range(16)] for c in range(2)]
PAIRS = [(i, i ^ 1) for i in range(32)]


def heat_kernel(gen, pts, own, other, part, tall, rows, horiz, ends, mid, cross, field, extra):
    lane = lax.broadcasted_iota(jnp.int32, (8, 128), 1)
    sub = lax.broadcasted_iota(jnp.int32, (8, 128), 0)
    half = lane >= 64
    block, place, core = position()
    strip = block * 16 + place

    for a in range(8):
        for q in range(16):
            tall[a, q, core] = own[q, a]
            tall[a, q, 1 - core] = other[q, a]
    flat = tall.reshape(8, 256, 128)
    zero = jnp.zeros((8, 128), jnp.float32)
    for i in range(LINES):
        field[0, i] = zero
        field[WIDE + 1, i] = zero
        horiz[WIDE, i] = zero

    scales = {1: HALF_DT, 6: DT, 7: -1.0}
    first_half = lax.broadcasted_iota(jnp.int32, (WIDE, 128), 1) < 64
    for a in (1, 2, 3, 4, 5, 6, 0, 7):
        for i in range(0, LINES, 2):
            pair = [flat[a, pl.ds(i + n, 64, stride=4), :] for n in range(2)]
            turned = jnp.concatenate(pair, axis=0).T
            if a in scales:
                turned = scales[a] * turned
            swapped = pltpu.roll(turned, 64, 1)
            rows[a, i] = jnp.where(first_half, turned, swapped)
            rows[a, i + 1] = jnp.where(first_half, swapped, turned)
            if a == 0:
                for n in range(2):
                    rows[a, i + n] += rows[6, i + n]

    weights = []
    for k in range(4):
        product = [lax.rem(pts[p] * gen[k], NLAT).astype(jnp.float32) / NLAT for p in range(4)]
        value = jnp.where(sub % 4 == 0, product[0], jnp.where(sub % 4 == 1, product[1], jnp.where(sub % 4 == 2, product[2], product[3])))
        found = []
        for y in range(4):
            line = flat[7, pl.ds(jnp.where(core == 0, SHIFT_ROWS[0][y], SHIFT_ROWS[1][y]), 1), :]
            found.append(jnp.broadcast_to(line[:, k : k + 1], (8, 128)))
        shift = jnp.where(half, jnp.where(sub < 4, found[2], found[3]), jnp.where(sub < 4, found[0], found[1]))
        value = value + shift
        value = value - jnp.floor(value)
        weights.append(0.5 - jnp.abs(2.0 * value - 1.0))

    def row(a, i, k):
        return jnp.broadcast_to(rows[a, i, pl.ds(k, 1), :], (8, 128))

    top = lane % 64 == 0
    bottom = lane % 64 == 63

    def coefs_at(k, left):
        c = []
        for i in range(LINES):
            e = (weights[0] * row(2, i, k) + weights[1] * row(3, i, k)) + (weights[2] * row(4, i, k) + weights[3] * row(5, i, k))
            c.append(row(1, i, k) * jnp.exp(e))
            horiz[k, i] = left[i] + c[i]
            field[k + 1, i] = row(0, i, k)
        for i in range(3):
            mid[k, i] = c[i] + c[i + 1]
        cross[k] = jnp.where(bottom, 0.0, c[3] + pltpu.roll(c[0], 127, 1))
        ends[k, 0] = jnp.where(top, 1.0 - c[0], 1.0)
        ends[k, 1] = jnp.where(bottom, 1.0 - c[3], 1.0)
        return tuple(c)

    lax.fori_loop(0, WIDE, coefs_at, (zero,) * LINES, unroll=16)

    def load(k):
        return tuple(field[k + 1, i] for i in range(LINES))

    def flux(k, u, right):
        return tuple(horiz[k + 1, i] * (right[i] - u[i]) for i in range(LINES))

    keep = {
        HALO - 1: jnp.where(strip == 0, 0.0, 1.0).astype(jnp.float32),
        WIDE - HALO: jnp.where(strip == 127, 0.0, 1.0).astype(jnp.float32),
    }

    def sweep(low, source, save):
        u = load(low)
        before = flux(low - 1, load(low - 1), u)
        for k in range(low, WIDE - low):
            right = load(k + 1)
            after = flux(k, u, right)
            down = [mid[k, i] * (u[i + 1] - u[i]) for i in range(3)]
            down.append(cross[k] * (pltpu.roll(u[0], 127, 1) - u[3]))
            wrapped = pltpu.roll(down[3], 1, 1)
            for i in range(LINES):
                y = (after[i] - before[i]) + (u[i] if 0 < i < 3 else ends[k, i // 3] * u[i])
                if source is not None:
                    y = y + source(k, i)
                y = (y + down[i]) - (down[i - 1] if i else wrapped)
                if k in keep:
                    y = y * keep[k]
                field[k + 1, i] = y
                if save:
                    extra[k, i] = y
            before, u = after, right

    def steps(first, last, source, save=False):
        while first <= last:
            times = min(GROUP, last - first + 1)

            def one(_, c, low=first):
                sweep(low, source, save)
                return c

            lax.fori_loop(0, times, one, 0)
            first += times

    control = lambda k, i: row(6, i, k)
    target = lambda k, i: row(7, i, k)
    misfit = lambda k, i: extra[k, i]

    steps(1, 15, control)
    steps(16, 16, target, True)

    def add_loss(k, total):
        return tuple(total[i] + extra[k, i] * extra[k, i] for i in range(LINES))

    loss = lax.fori_loop(HALO, HALO + CORE, add_loss, (zero,) * LINES, unroll=8)
    loss = jnp.sum((loss[0] + loss[1]) + (loss[2] + loss[3]), axis=(0, 1), keepdims=True)
    last = 16
    for power in (8, 4, 2, 1):
        steps(last + 1, last + power - 1, None)
        last += power
        steps(last, last, misfit, power > 1)
    steps(32, 32, None)

    inner = flat[6, :, HALO : HALO + CORE]
    squares = 0.5 * jnp.sum(inner * inner, axis=(0, 1), keepdims=True)
    wide_lane = lax.broadcasted_iota(jnp.int32, (256, CORE), 1)
    part[:, CORE:] = jnp.where(wide_lane == 0, loss, jnp.where(wide_lane == 1, squares, 0.0))
    part[:, :CORE] = 0.25 * inner
    for i in range(LINES):
        total = jnp.sum(field[pl.ds(HALO + 1, CORE), i], axis=1)
        total = (total + pltpu.roll(total, 64, 1)) * (DT / 32)
        part[pl.ds(i, 64, stride=4), :] += jnp.concatenate([total.T[:64], jnp.zeros((64, CORE), jnp.float32)], axis=1)


def heat(gen, pts, own, other):
    smem = pl.BlockSpec(memory_space=pltpu.SMEM)
    vmem = pl.BlockSpec(memory_space=pltpu.VMEM)
    f32 = jnp.float32
    return pl.pallas_call(
        heat_kernel,
        out_shape=jax.ShapeDtypeStruct((256, 128), f32),
        in_specs=[smem, smem, vmem, vmem],
        out_specs=vmem,
        scratch_shapes=[
            pltpu.VMEM((8, 16, 2, 8, 128), f32),
            pltpu.VMEM((8, LINES, WIDE, 128), f32),
            pltpu.VMEM((WIDE + 1, LINES, 8, 128), f32),
            pltpu.VMEM((WIDE, 2, 8, 128), f32),
            pltpu.VMEM((WIDE, 3, 8, 128), f32),
            pltpu.VMEM((WIDE, 8, 128), f32),
            pltpu.VMEM((WIDE + 2, LINES, 8, 128), f32),
            pltpu.VMEM((WIDE, LINES, 8, 128), f32),
        ],
        compiler_params=pltpu.CompilerParams(vmem_limit_bytes=48 * 2**20),
    )(gen, pts, own, other)


def pack_kernel(shifts, start, base, modes, control, target, pieces, window, packed, vector_of, sems, out_sems, shift_sem):
    block = position()[0]
    shift_copy = pltpu.make_async_copy(shifts, vector_of, shift_sem)
    shift_copy.start()
    column = pl.multiple_of(block * 1024, 1024)
    before = pl.multiple_of(jnp.maximum(column - 128, 0), 128)
    after = pl.multiple_of(jnp.minimum(column + 1024, 8192 - 128), 128)
    sources = ((start, 0), (base, 1), (control, 6), (target, 7), (modes, slice(2, 6)))
    copies = []
    for n, (source, a) in enumerate(sources):
        group = []
        for part, (begin, to, length) in enumerate(((before, 0, 128), (column, 128, 1024), (after, 1152, 128))):
            group.append(
                pltpu.make_async_copy(
                    source.at[..., pl.ds(begin, length)], window.at[a, :, pl.ds(to, length)], sems.at[n, part]
                )
            )
            group[-1].start()
        copies.append(group)
    shift_copy.wait()
    lane = lax.broadcasted_iota(jnp.int32, (8, 128), 1)
    vector = jnp.zeros((8, 128), jnp.float32)
    for m in range(4):
        vector = jnp.where(lane == m, vector_of[0, m], vector)
    inside = {
        0: jnp.logical_or(lane >= HALO, block > 0),
        15: jnp.logical_or(lane < WIDE - HALO, block < 7),
    }
    sends = []
    for group, arrays in zip(copies, ((0,), (1,), (6,), (7,), (2, 3, 4, 5))):
        for copy in group:
            copy.wait()
        for a in arrays:
            for q in range(16):
                piece = window[a, :, 96 + 64 * q : 224 + 64 * q]
                if q in inside:
                    piece = jnp.where(inside[q], piece, 0.0)
                if a == 7:
                    piece = jnp.where(lane < 4, vector, piece)
                packed[a, q] = piece
            sends.append(pltpu.make_async_copy(packed.at[a], pieces.at[:, a], out_sems.at[a]))
            sends[-1].start()
    for send in sends:
        send.wait()


def pack(shifts, start, base, modes, control, target):
    hbm = pl.BlockSpec(memory_space=pltpu.HBM)
    f32 = jnp.float32
    return pl.pallas_call(
        pack_kernel,
        out_shape=jax.ShapeDtypeStruct((16, 8, 8, 128), f32),
        in_specs=[hbm] * 6,
        out_specs=hbm,
        scratch_shapes=[
            pltpu.VMEM((8, 8, 1280), f32),
            pltpu.VMEM((8, 16, 8, 128), f32),
            pltpu.SMEM((1, 4), f32),
            pltpu.SemaphoreType.DMA((5, 3)),
            pltpu.SemaphoreType.DMA((8,)),
            pltpu.SemaphoreType.DMA,
        ],
        compiler_params=pltpu.CompilerParams(vmem_limit_bytes=60 * 2**20),
    )(shifts, start, base, modes, control, target)


def spread_kernel(own, other, pieces, total):
    core = position()[2]
    total[...] = own[...] + other[...]
    lane = lax.broadcasted_iota(jnp.int32, (256, 128), 1)
    gradient = jnp.where(lane < CORE, total[...], 0.0)
    squares = jnp.sum(gradient * gradient, axis=(0, 1), keepdims=True)
    stats = pltpu.roll(total[:1], 64, 1)
    stats = jnp.where(lane[:1] < 2, stats, jnp.where(lane[:1] == 2, squares, 0.0))
    left = lane[:4] < CORE
    for q in range(16):
        rows = total[pl.ds(pl.multiple_of(16 * q + 8 * core, 8), 8), :]
        packed = jnp.where(left, rows[:4], pltpu.roll(rows[4:], 64, 1))
        for b in range(8):
            pieces[pl.ds(PIECE * (16 * b + q), 4), :] = packed
            pieces[pl.ds(PIECE * (16 * b + q) + 4, 1), :] = stats


def spread(own, other):
    vmem = pl.BlockSpec(memory_space=pltpu.VMEM)
    return pl.pallas_call(
        spread_kernel,
        out_shape=jax.ShapeDtypeStruct((128 * PIECE, 128), jnp.float32),
        in_specs=[vmem, vmem],
        out_specs=vmem,
        scratch_shapes=[pltpu.VMEM((256, 128), jnp.float32)],
        compiler_params=pltpu.CompilerParams(vmem_limit_bytes=8 * 2**20),
    )(own, other)


def finish_kernel(pieces, control, updated, objective):
    sums = [pieces[pl.ds(4 + i, 32, stride=4 * PIECE), :] for i in range(0, 4 * PIECE, PIECE)]
    stats = jnp.sum((sums[0] + sums[1]) + (sums[2] + sums[3]), axis=0, keepdims=True)
    lane = lax.broadcasted_iota(jnp.int32, (1, 128), 1)

    def entry(n):
        return jnp.sum(jnp.where(lane == n, stats, 0.0), axis=(0, 1), keepdims=True)

    cells = 256 * 8192
    objective[...] = (entry(0) * (0.5 / 32) + entry(1) * 0.25) / cells
    scaling = jnp.broadcast_to(0.5 / jnp.sqrt(entry(2) / cells + 1e-06), (4, 128))
    left = lax.broadcasted_iota(jnp.int32, (4, 128), 1) < CORE
    for n in range(64):
        columns = slice(128 * n, 128 * (n + 1))
        one, two = (pieces[pl.ds(PIECE * (2 * n + i), 4), :] for i in range(2))
        updated[:4, columns] = control[:4, columns] - scaling * jnp.where(left, one, pltpu.roll(two, 64, 1))
        updated[4:, columns] = control[4:, columns] - scaling * jnp.where(left, pltpu.roll(one, 64, 1), two)


def finish(pieces, control):
    vmem = pl.BlockSpec(memory_space=pltpu.VMEM)
    return pl.pallas_call(
        finish_kernel,
        out_shape=(jax.ShapeDtypeStruct((8, 8192), jnp.float32), jax.ShapeDtypeStruct((1, 1), jnp.float32)),
        in_specs=[vmem, vmem],
        out_specs=(vmem, vmem),
        compiler_params=pltpu.CompilerParams(vmem_limit_bytes=8 * 2**20),
    )(pieces, control)


def local(start_state, base_field, modes, control, target, shifts, gen_vector, point_ids):
    sent = pack(shifts, start_state, base_field, modes, control, target)
    own = lax.all_to_all(sent, LINKS, 0, 0, axis_index_groups=BLOCK_GROUPS, tiled=True)
    other = lax.ppermute(own, "slab", PAIRS)
    part = heat(gen_vector, point_ids, own, other)
    pieces = spread(part, lax.ppermute(part, "slab", PAIRS))
    pieces = pieces.reshape(128, 1, PIECE * 128)
    pieces = lax.all_to_all(pieces, LINKS, 0, 0, axis_index_groups=CORE_GROUPS, tiled=True)
    pieces = pieces.reshape(128 * PIECE, 128)
    new_control, objective = finish(pieces, control)
    return new_control, objective[0, 0]


def solution(mesh):
    return jax.shard_map(
        local,
        mesh=mesh,
        in_specs=(
            P("slab", None),
            P("slab", None),
            P(None, "slab", None),
            P("slab", None),
            P("slab", None),
            P("shift", None),
            P(),
            P(),
        ),
        out_specs=(P("slab", None), P()),
        check_vma=False,
    )
```

```python
import jax
import jax.numpy as jnp
from jax import lax
from jax.experimental import pallas as pl
from jax.experimental.pallas import tpu as pltpu
from jax.sharding import PartitionSpec as P

NLAT = 1021
HALF_DT = 0.02
DT = 0.04
HALO = 32
WIDE = 128
CORE = 64
LINES = 4
GROUP = 4
PIECE = 5
LINKS = ("shift", "slab")


X_OFF = (2, 1, 0, 1, 3, 2, 3, 0, 3, 0, 3, 2, 0, 1, 2, 1)
X_BITS = sum(x << (2 * q) for q, x in enumerate(X_OFF[:8])), sum(x << (2 * q) for q, x in enumerate(X_OFF[8:]))
SHIFT_ROWS = tuple(tuple(16 * (8 * c + X_OFF[8 * c : 8 * c + 8].index(x)) for x in range(4)) for c in range(2))


def position():
    shift, slab = lax.axis_index("shift"), lax.axis_index("slab")
    z_low, y, core = lax.div(slab, 8), lax.rem(lax.div(slab, 2), 4), lax.rem(slab, 2)
    z_high, x = lax.div(shift, 4), lax.rem(shift, 4)
    place = z_low * 4 + y
    bits = jnp.where(place < 8, X_BITS[0], X_BITS[1])
    offset = lax.rem(lax.shift_right_logical(bits, 2 * lax.rem(place, 8)), 4)
    block = lax.rem(z_high + 1 - lax.div(z_low, 2), 2) * 4 + lax.rem(x - offset + 4, 4)
    return block, place, core


def device_at(block, place, core):
    z_low, y = divmod(place, 4)
    z_high, x = divmod(block, 4)
    return ((z_high ^ (1 - z_low // 2)) * 4 + (x + X_OFF[place]) % 4) * 32 + z_low * 8 + y * 2 + core


BLOCK_GROUPS = [[device_at(b, q, c) for q in range(16)] for b in range(8) for c in range(2)]
CORE_GROUPS = [[device_at(b, q, c) for b in range(8) for q in range(16)] for c in range(2)]
PAIRS = [(i, i ^ 1) for i in range(32)]


def heat_kernel(gen, pts, own, other, part, tall, rows, horiz, ends, mid, cross, field, extra):
    lane = lax.broadcasted_iota(jnp.int32, (8, 128), 1)
    sub = lax.broadcasted_iota(jnp.int32, (8, 128), 0)
    half = lane >= 64
    block, place, core = position()
    strip = block * 16 + place

    for a in range(8):
        for q in range(16):
            tall[a, q, core] = own[q, a]
            tall[a, q, 1 - core] = other[q, a]
    flat = tall.reshape(8, 256, 128)
    zero = jnp.zeros((8, 128), jnp.float32)
    for i in range(LINES):
        field[0, i] = zero
        field[WIDE + 1, i] = zero
        horiz[WIDE, i] = zero

    scales = {1: HALF_DT, 6: DT, 7: -1.0}
    first_half = lax.broadcasted_iota(jnp.int32, (WIDE, 128), 1) < 64
    for a in (1, 2, 3, 4, 5, 6, 0, 7):
        for i in range(0, LINES, 2):
            pair = [flat[a, pl.ds(i + n, 64, stride=4), :] for n in range(2)]
            turned = jnp.concatenate(pair, axis=0).T
            if a in scales:
                turned = scales[a] * turned
            swapped = pltpu.roll(turned, 64, 1)
            rows[a, i] = jnp.where(first_half, turned, swapped)
            rows[a, i + 1] = jnp.where(first_half, swapped, turned)
            if a == 0:
                for n in range(2):
                    rows[a, i + n] += rows[6, i + n]

    weights = []
    for k in range(4):
        product = [lax.rem(pts[p] * gen[k], NLAT).astype(jnp.float32) / NLAT for p in range(4)]
        value = jnp.where(sub % 4 == 0, product[0], jnp.where(sub % 4 == 1, product[1], jnp.where(sub % 4 == 2, product[2], product[3])))
        found = []
        for y in range(4):
            line = flat[7, pl.ds(jnp.where(core == 0, SHIFT_ROWS[0][y], SHIFT_ROWS[1][y]), 1), :]
            found.append(jnp.broadcast_to(line[:, k : k + 1], (8, 128)))
        shift = jnp.where(half, jnp.where(sub < 4, found[2], found[3]), jnp.where(sub < 4, found[0], found[1]))
        value = value + shift
        value = value - jnp.floor(value)
        weights.append(0.5 - jnp.abs(2.0 * value - 1.0))

    def row(a, i, k):
        return jnp.broadcast_to(rows[a, i, pl.ds(k, 1), :], (8, 128))

    top = lane % 64 == 0
    bottom = lane % 64 == 63

    def coefs_at(k, left):
        c = []
        for i in range(LINES):
            e = (weights[0] * row(2, i, k) + weights[1] * row(3, i, k)) + (weights[2] * row(4, i, k) + weights[3] * row(5, i, k))
            c.append(row(1, i, k) * jnp.exp(e))
            horiz[k, i] = left[i] + c[i]
            field[k + 1, i] = row(0, i, k)
        for i in range(3):
            mid[k, i] = c[i] + c[i + 1]
        over, under = pltpu.roll(c[3], 1, 1), pltpu.roll(c[0], 127, 1)
        cross[k, 0] = jnp.where(top, 0.0, c[0] + over)
        cross[k, 1] = jnp.where(bottom, 0.0, c[3] + under)
        ends[k, 0] = 1.0 - jnp.where(top, c[0], c[0] + over)
        ends[k, 1] = 1.0 - jnp.where(bottom, c[3], c[3] + under)
        return tuple(c)

    lax.fori_loop(0, WIDE, coefs_at, (zero,) * LINES, unroll=64)

    def load(k):
        return tuple(field[k + 1, i] for i in range(LINES))

    def flux(k, u, right):
        return tuple(horiz[k + 1, i] * (right[i] - u[i]) for i in range(LINES))

    keep = {
        HALO - 1: jnp.where(strip == 0, 0.0, 1.0).astype(jnp.float32),
        WIDE - HALO: jnp.where(strip == 127, 0.0, 1.0).astype(jnp.float32),
    }

    def sweep(low, source, save):
        u = load(low)
        before = flux(low - 1, load(low - 1), u)
        for k in range(low, WIDE - low):
            right = load(k + 1)
            after = flux(k, u, right)
            down = [mid[k, i] * (u[i + 1] - u[i]) for i in range(3)]
            over, under = cross[k, 0] * pltpu.roll(u[3], 1, 1), cross[k, 1] * pltpu.roll(u[0], 127, 1)
            for i in range(LINES):
                y = (after[i] - before[i]) + (u[i] if 0 < i < 3 else ends[k, i // 3] * u[i])
                if source is not None:
                    y = y + source(k, i)
                y = y + (down[i] if i < 3 else under)
                y = y - down[i - 1] if i else y + over
                if k in keep:
                    y = y * keep[k]
                field[k + 1, i] = y
                if save:
                    extra[k, i] = y
            before, u = after, right

    def steps(first, last, source, save=False):
        while first <= last:
            times = min(GROUP, last - first + 1)

            def one(_, c, low=first):
                sweep(low, source, save)
                return c

            lax.fori_loop(0, times, one, 0)
            first += times

    control = lambda k, i: row(6, i, k)
    target = lambda k, i: row(7, i, k)
    misfit = lambda k, i: extra[k, i]

    steps(1, 15, control)
    steps(16, 16, target, True)

    def add_loss(k, total):
        return tuple(total[i] + extra[k, i] * extra[k, i] for i in range(LINES))

    loss = lax.fori_loop(HALO, HALO + CORE, add_loss, (zero,) * LINES, unroll=64)
    loss = jnp.sum((loss[0] + loss[1]) + (loss[2] + loss[3]), axis=(0, 1), keepdims=True)
    last = 16
    for power in (8, 4, 2, 1):
        steps(last + 1, last + power - 1, None)
        last += power
        steps(last, last, misfit, power > 1)
    steps(32, 32, None)

    inner = flat[6, :, HALO : HALO + CORE]
    squares = 0.5 * jnp.sum(inner * inner, axis=(0, 1), keepdims=True)
    wide_lane = lax.broadcasted_iota(jnp.int32, (256, CORE), 1)
    part[:, CORE:] = jnp.where(wide_lane == 0, loss, jnp.where(wide_lane == 1, squares, 0.0))
    part[:, :CORE] = 0.25 * inner
    for i in range(LINES):
        total = jnp.sum(field[pl.ds(HALO + 1, CORE), i], axis=1)
        total = (total + pltpu.roll(total, 64, 1)) * (DT / 32)
        part[pl.ds(i, 64, stride=4), :] += jnp.concatenate([total.T[:64], jnp.zeros((64, CORE), jnp.float32)], axis=1)


def heat(gen, pts, own, other):
    smem = pl.BlockSpec(memory_space=pltpu.SMEM)
    vmem = pl.BlockSpec(memory_space=pltpu.VMEM)
    f32 = jnp.float32
    return pl.pallas_call(
        heat_kernel,
        out_shape=jax.ShapeDtypeStruct((256, 128), f32),
        in_specs=[smem, smem, vmem, vmem],
        out_specs=vmem,
        scratch_shapes=[
            pltpu.VMEM((8, 16, 2, 8, 128), f32),
            pltpu.VMEM((8, LINES, WIDE, 128), f32),
            pltpu.VMEM((WIDE + 1, LINES, 8, 128), f32),
            pltpu.VMEM((WIDE, 2, 8, 128), f32),
            pltpu.VMEM((WIDE, 3, 8, 128), f32),
            pltpu.VMEM((WIDE, 2, 8, 128), f32),
            pltpu.VMEM((WIDE + 2, LINES, 8, 128), f32),
            pltpu.VMEM((WIDE, LINES, 8, 128), f32),
        ],
        compiler_params=pltpu.CompilerParams(vmem_limit_bytes=48 * 2**20),
    )(gen, pts, own, other)


def pack_kernel(shifts, start, base, modes, control, target, pieces, window, packed, vector_of, sems, out_sems, shift_sem):
    block = position()[0]
    shift_copy = pltpu.make_async_copy(shifts, vector_of, shift_sem)
    shift_copy.start()
    column = block * 1024
    begin = pl.multiple_of(jnp.clip(column - 128, 0, 8192 - 1280), 128)
    ahead = pl.multiple_of(column - begin, 128)
    sources = ((start, 0), (base, 1), (control, 6), (target, 7), (modes, slice(2, 6)))
    copies = []
    for n, (source, a) in enumerate(sources):
        copy = pltpu.make_async_copy(source.at[..., pl.ds(begin, 1280)], window.at[a, :, 128:1408], sems.at[n])
        copy.start()
        copies.append(copy)
    shift_copy.wait()
    lane = lax.broadcasted_iota(jnp.int32, (8, 128), 1)
    vector = jnp.zeros((8, 128), jnp.float32)
    for m in range(4):
        vector = jnp.where(lane == m, vector_of[0, m], vector)
    inside = {
        0: jnp.logical_or(lane >= HALO, block > 0),
        15: jnp.logical_or(lane < WIDE - HALO, block < 7),
    }
    sends = []
    for group, arrays in zip(copies, ((0,), (1,), (6,), (7,), (2, 3, 4, 5))):
        group.wait()
        for a in arrays:
            for q in range(16):
                two = window[a, :, pl.ds(pl.multiple_of(ahead + 128 * ((q + 1) // 2), 128), 256)]
                piece = two[:, 32:160] if q % 2 else two[:, 96:224]
                if q in inside:
                    piece = jnp.where(inside[q], piece, 0.0)
                if a == 7:
                    piece = jnp.where(lane < 4, vector, piece)
                packed[a, q] = piece
            sends.append(pltpu.make_async_copy(packed.at[a], pieces.at[:, a], out_sems.at[a]))
            sends[-1].start()
    for send in sends:
        send.wait()


def pack(shifts, start, base, modes, control, target):
    hbm = pl.BlockSpec(memory_space=pltpu.HBM)
    f32 = jnp.float32
    return pl.pallas_call(
        pack_kernel,
        out_shape=jax.ShapeDtypeStruct((16, 8, 8, 128), f32),
        in_specs=[hbm] * 6,
        out_specs=hbm,
        scratch_shapes=[
            pltpu.VMEM((8, 8, 1536), f32),
            pltpu.VMEM((8, 16, 8, 128), f32),
            pltpu.SMEM((1, 4), f32),
            pltpu.SemaphoreType.DMA((5,)),
            pltpu.SemaphoreType.DMA((8,)),
            pltpu.SemaphoreType.DMA,
        ],
        compiler_params=pltpu.CompilerParams(vmem_limit_bytes=60 * 2**20),
    )(shifts, start, base, modes, control, target)


def spread_kernel(own, other, pieces, total):
    core = position()[2]
    total[...] = own[...] + other[...]
    lane = lax.broadcasted_iota(jnp.int32, (256, 128), 1)
    gradient = jnp.where(lane < CORE, total[...], 0.0)
    squares = jnp.sum(gradient * gradient, axis=(0, 1), keepdims=True)
    stats = pltpu.roll(total[:1], 64, 1)
    stats = jnp.where(lane[:1] < 2, stats, jnp.where(lane[:1] == 2, squares, 0.0))
    left = lane[:4] < CORE
    for q in range(16):
        rows = total[pl.ds(pl.multiple_of(16 * q + 8 * core, 8), 8), :]
        packed = jnp.where(left, rows[:4], pltpu.roll(rows[4:], 64, 1))
        for b in range(8):
            pieces[pl.ds(PIECE * (16 * b + q), 4), :] = packed
            pieces[pl.ds(PIECE * (16 * b + q) + 4, 1), :] = stats


def spread(own, other):
    vmem = pl.BlockSpec(memory_space=pltpu.VMEM)
    return pl.pallas_call(
        spread_kernel,
        out_shape=jax.ShapeDtypeStruct((128 * PIECE, 128), jnp.float32),
        in_specs=[vmem, vmem],
        out_specs=vmem,
        scratch_shapes=[pltpu.VMEM((256, 128), jnp.float32)],
        compiler_params=pltpu.CompilerParams(vmem_limit_bytes=8 * 2**20),
    )(own, other)


def finish_kernel(pieces, control, updated, objective):
    sums = [pieces[pl.ds(4 + i, 32, stride=4 * PIECE), :] for i in range(0, 4 * PIECE, PIECE)]
    stats = jnp.sum((sums[0] + sums[1]) + (sums[2] + sums[3]), axis=0, keepdims=True)
    lane = lax.broadcasted_iota(jnp.int32, (1, 128), 1)

    def entry(n):
        return jnp.sum(jnp.where(lane == n, stats, 0.0), axis=(0, 1), keepdims=True)

    cells = 256 * 8192
    objective[...] = (entry(0) * (0.5 / 32) + entry(1) * 0.25) / cells
    scaling = jnp.broadcast_to(0.5 / jnp.sqrt(entry(2) / cells + 1e-06), (4, 128))
    left = lax.broadcasted_iota(jnp.int32, (4, 128), 1) < CORE
    for n in range(64):
        columns = slice(128 * n, 128 * (n + 1))
        one, two = (pieces[pl.ds(PIECE * (2 * n + i), 4), :] for i in range(2))
        updated[:4, columns] = control[:4, columns] - scaling * jnp.where(left, one, pltpu.roll(two, 64, 1))
        updated[4:, columns] = control[4:, columns] - scaling * jnp.where(left, pltpu.roll(one, 64, 1), two)


def finish(pieces, control):
    vmem = pl.BlockSpec(memory_space=pltpu.VMEM)
    return pl.pallas_call(
        finish_kernel,
        out_shape=(jax.ShapeDtypeStruct((8, 8192), jnp.float32), jax.ShapeDtypeStruct((1, 1), jnp.float32)),
        in_specs=[vmem, vmem],
        out_specs=(vmem, vmem),
        compiler_params=pltpu.CompilerParams(vmem_limit_bytes=8 * 2**20),
    )(pieces, control)


def local(start_state, base_field, modes, control, target, shifts, gen_vector, point_ids):
    sent = pack(shifts, start_state, base_field, modes, control, target)
    own = lax.all_to_all(sent, LINKS, 0, 0, axis_index_groups=BLOCK_GROUPS, tiled=True)
    other = lax.ppermute(own, "slab", PAIRS)
    part = heat(gen_vector, point_ids, own, other)
    pieces = spread(part, lax.ppermute(part, "slab", PAIRS))
    pieces = pieces.reshape(128, 1, PIECE * 128)
    pieces = lax.all_to_all(pieces, LINKS, 0, 0, axis_index_groups=CORE_GROUPS, tiled=True)
    pieces = pieces.reshape(128 * PIECE, 128)
    new_control, objective = finish(pieces, control)
    return new_control, objective[0, 0]


def solution(mesh):
    return jax.shard_map(
        local,
        mesh=mesh,
        in_specs=(
            P("slab", None),
            P("slab", None),
            P(None, "slab", None),
            P("slab", None),
            P("slab", None),
            P("shift", None),
            P(),
            P(),
        ),
        out_specs=(P("slab", None), P()),
        check_vma=False,
    )
```

```python
import jax
import jax.numpy as jnp
from jax import lax
from jax.experimental import pallas as pl
from jax.experimental.pallas import tpu as pltpu
from jax.sharding import PartitionSpec as P

NLAT = 1021
HALF_DT = 0.02
DT = 0.04
HALO = 32
WIDE = 128
CORE = 64
LINES = 4
GROUP = 4
PIECE = 5
LINKS = ("shift", "slab")


X_OFF = (2, 1, 0, 1, 3, 2, 3, 0, 3, 0, 3, 2, 0, 1, 2, 1)
X_BITS = sum(x << (2 * q) for q, x in enumerate(X_OFF[:8])), sum(x << (2 * q) for q, x in enumerate(X_OFF[8:]))
SHIFT_ROWS = tuple(tuple(16 * (8 * c + X_OFF[8 * c : 8 * c + 8].index(x)) for x in range(4)) for c in range(2))


def position():
    shift, slab = lax.axis_index("shift"), lax.axis_index("slab")
    z_low, y, core = lax.div(slab, 8), lax.rem(lax.div(slab, 2), 4), lax.rem(slab, 2)
    z_high, x = lax.div(shift, 4), lax.rem(shift, 4)
    place = z_low * 4 + y
    bits = jnp.where(place < 8, X_BITS[0], X_BITS[1])
    offset = lax.rem(lax.shift_right_logical(bits, 2 * lax.rem(place, 8)), 4)
    block = lax.rem(z_high + 1 - lax.div(z_low, 2), 2) * 4 + lax.rem(x - offset + 4, 4)
    return block, place, core


def device_at(block, place, core):
    z_low, y = divmod(place, 4)
    z_high, x = divmod(block, 4)
    return ((z_high ^ (1 - z_low // 2)) * 4 + (x + X_OFF[place]) % 4) * 32 + z_low * 8 + y * 2 + core


SLOTS = (0, 1, 2, 3, 12, 13, 14, 15, 4, 5, 6, 7, 8, 9, 10, 11)
BLOCK_GROUPS = [[device_at(b, q, c) for q in SLOTS] for b in range(8) for c in range(2)]
CORE_GROUPS = [[device_at(b, q, c) for b in range(8) for q in range(16)] for c in range(2)]
PAIRS = [(i, i ^ 1) for i in range(32)]


def heat_kernel(gen, pts, own, other, part, tall, rows, horiz, ends, mid, cross, field, extra):
    lane = lax.broadcasted_iota(jnp.int32, (8, 128), 1)
    sub = lax.broadcasted_iota(jnp.int32, (8, 128), 0)
    half = lane >= 64
    block, place, core = position()
    strip = block * 16 + place

    for a in range(8):
        for n, q in enumerate(SLOTS):
            tall[a, q, core] = own[n, a]
            tall[a, q, 1 - core] = other[n, a]
    flat = tall.reshape(8, 256, 128)
    zero = jnp.zeros((8, 128), jnp.float32)
    for i in range(LINES):
        field[0, i] = zero
        field[WIDE + 1, i] = zero
        horiz[WIDE, i] = zero

    scales = {1: HALF_DT, 6: DT, 7: -1.0}
    first_half = lax.broadcasted_iota(jnp.int32, (WIDE, 128), 1) < 64
    for a in (1, 2, 3, 4, 5, 6, 0, 7):
        for i in range(0, LINES, 2):
            pair = [flat[a, pl.ds(i + n, 64, stride=4), :] for n in range(2)]
            turned = jnp.concatenate(pair, axis=0).T
            if a in scales:
                turned = scales[a] * turned
            swapped = pltpu.roll(turned, 64, 1)
            rows[a, i] = jnp.where(first_half, turned, swapped)
            rows[a, i + 1] = jnp.where(first_half, swapped, turned)
            if a == 0:
                for n in range(2):
                    rows[a, i + n] += rows[6, i + n]

    weights = []
    for k in range(4):
        product = [lax.rem(pts[p] * gen[k], NLAT).astype(jnp.float32) / NLAT for p in range(4)]
        value = jnp.where(sub % 4 == 0, product[0], jnp.where(sub % 4 == 1, product[1], jnp.where(sub % 4 == 2, product[2], product[3])))
        found = []
        for y in range(4):
            line = flat[7, pl.ds(jnp.where(core == 0, SHIFT_ROWS[0][y], SHIFT_ROWS[1][y]), 1), :]
            found.append(jnp.broadcast_to(line[:, k : k + 1], (8, 128)))
        shift = jnp.where(half, jnp.where(sub < 4, found[2], found[3]), jnp.where(sub < 4, found[0], found[1]))
        value = value + shift
        value = value - jnp.floor(value)
        weights.append(0.5 - jnp.abs(2.0 * value - 1.0))

    def row(a, i, k):
        return jnp.broadcast_to(rows[a, i, pl.ds(k, 1), :], (8, 128))

    top = lane % 64 == 0
    bottom = lane % 64 == 63

    def coefs_at(k, left):
        c = []
        for i in range(LINES):
            e = (weights[0] * row(2, i, k) + weights[1] * row(3, i, k)) + (weights[2] * row(4, i, k) + weights[3] * row(5, i, k))
            c.append(row(1, i, k) * jnp.exp(e))
            horiz[k, i] = left[i] + c[i]
            field[k + 1, i] = row(0, i, k)
        for i in range(3):
            mid[k, i] = c[i] + c[i + 1]
        over, under = pltpu.roll(c[3], 1, 1), pltpu.roll(c[0], 127, 1)
        cross[k, 0] = jnp.where(top, 0.0, c[0] + over)
        cross[k, 1] = jnp.where(bottom, 0.0, c[3] + under)
        ends[k, 0] = 1.0 - jnp.where(top, c[0], c[0] + over)
        ends[k, 1] = 1.0 - jnp.where(bottom, c[3], c[3] + under)
        return tuple(c)

    lax.fori_loop(0, WIDE, coefs_at, (zero,) * LINES, unroll=64)

    def load(k):
        return tuple(field[k + 1, i] for i in range(LINES))

    def flux(k, u, right):
        return tuple(horiz[k + 1, i] * (right[i] - u[i]) for i in range(LINES))

    keep = {
        HALO - 1: jnp.where(strip == 0, 0.0, 1.0).astype(jnp.float32),
        WIDE - HALO: jnp.where(strip == 127, 0.0, 1.0).astype(jnp.float32),
    }

    def sweep(low, source, save):
        u = load(low)
        before = flux(low - 1, load(low - 1), u)
        for k in range(low, WIDE - low):
            right = load(k + 1)
            after = flux(k, u, right)
            down = [mid[k, i] * (u[i + 1] - u[i]) for i in range(3)]
            over, under = cross[k, 0] * pltpu.roll(u[3], 1, 1), cross[k, 1] * pltpu.roll(u[0], 127, 1)
            for i in range(LINES):
                y = (after[i] - before[i]) + (u[i] if 0 < i < 3 else ends[k, i // 3] * u[i])
                if source is not None:
                    y = y + source(k, i)
                y = y + (down[i] if i < 3 else under)
                y = y - down[i - 1] if i else y + over
                if k in keep:
                    y = y * keep[k]
                field[k + 1, i] = y
                if save:
                    extra[k, i] = y
            before, u = after, right

    def steps(first, last, source, save=False):
        while first <= last:
            times = min(GROUP, last - first + 1)

            def one(_, c, low=first):
                sweep(low, source, save)
                return c

            lax.fori_loop(0, times, one, 0)
            first += times

    control = lambda k, i: row(6, i, k)
    target = lambda k, i: row(7, i, k)
    misfit = lambda k, i: extra[k, i]

    steps(1, 15, control)
    steps(16, 16, target, True)

    def add_loss(k, total):
        return tuple(total[i] + extra[k, i] * extra[k, i] for i in range(LINES))

    loss = lax.fori_loop(HALO, HALO + CORE, add_loss, (zero,) * LINES, unroll=64)
    loss = jnp.sum((loss[0] + loss[1]) + (loss[2] + loss[3]), axis=(0, 1), keepdims=True)
    last = 16
    for power in (8, 4, 2, 1):
        steps(last + 1, last + power - 1, None)
        last += power
        steps(last, last, misfit, power > 1)
    steps(32, 32, None)

    inner = flat[6, :, HALO : HALO + CORE]
    squares = 0.5 * jnp.sum(inner * inner, axis=(0, 1), keepdims=True)
    wide_lane = lax.broadcasted_iota(jnp.int32, (256, CORE), 1)
    part[:, CORE:] = jnp.where(wide_lane == 0, loss, jnp.where(wide_lane == 1, squares, 0.0))
    part[:, :CORE] = 0.25 * inner
    for i in range(LINES):
        total = jnp.sum(field[pl.ds(HALO + 1, CORE), i], axis=1)
        total = (total + pltpu.roll(total, 64, 1)) * (DT / 32)
        part[pl.ds(i, 64, stride=4), :] += jnp.concatenate([total.T[:64], jnp.zeros((64, CORE), jnp.float32)], axis=1)


def heat(gen, pts, own, other):
    smem = pl.BlockSpec(memory_space=pltpu.SMEM)
    vmem = pl.BlockSpec(memory_space=pltpu.VMEM)
    f32 = jnp.float32
    return pl.pallas_call(
        heat_kernel,
        out_shape=jax.ShapeDtypeStruct((256, 128), f32),
        in_specs=[smem, smem, vmem, vmem],
        out_specs=vmem,
        scratch_shapes=[
            pltpu.VMEM((8, 16, 2, 8, 128), f32),
            pltpu.VMEM((8, LINES, WIDE, 128), f32),
            pltpu.VMEM((WIDE + 1, LINES, 8, 128), f32),
            pltpu.VMEM((WIDE, 2, 8, 128), f32),
            pltpu.VMEM((WIDE, 3, 8, 128), f32),
            pltpu.VMEM((WIDE, 2, 8, 128), f32),
            pltpu.VMEM((WIDE + 2, LINES, 8, 128), f32),
            pltpu.VMEM((WIDE, LINES, 8, 128), f32),
        ],
        compiler_params=pltpu.CompilerParams(vmem_limit_bytes=48 * 2**20),
    )(gen, pts, own, other)


def pack_kernel(shifts, start, base, modes, control, target, pieces, window, packed, vector_of, sems, out_sems, shift_sem):
    block = position()[0]
    shift_copy = pltpu.make_async_copy(shifts, vector_of, shift_sem)
    shift_copy.start()
    column = block * 1024
    begin = pl.multiple_of(jnp.clip(column - 128, 0, 8192 - 1280), 128)
    ahead = pl.multiple_of(column - begin, 128)
    sources = ((start, 0), (base, 1), (control, 6), (target, 7), (modes, slice(2, 6)))
    copies = []
    for n, (source, a) in enumerate(sources):
        copy = pltpu.make_async_copy(source.at[..., pl.ds(begin, 1280)], window.at[a, :, 128:1408], sems.at[n])
        copy.start()
        copies.append(copy)
    shift_copy.wait()
    lane = lax.broadcasted_iota(jnp.int32, (8, 128), 1)
    vector = jnp.zeros((8, 128), jnp.float32)
    for m in range(4):
        vector = jnp.where(lane == m, vector_of[0, m], vector)
    inside = {
        0: jnp.logical_or(lane >= HALO, block > 0),
        15: jnp.logical_or(lane < WIDE - HALO, block < 7),
    }
    sends = []
    for group, arrays in zip(copies, ((0,), (1,), (6,), (7,), (2, 3, 4, 5))):
        group.wait()
        for a in arrays:
            for q in range(16):
                two = window[a, :, pl.ds(pl.multiple_of(ahead + 128 * ((q + 1) // 2), 128), 256)]
                piece = two[:, 32:160] if q % 2 else two[:, 96:224]
                if q in inside:
                    piece = jnp.where(inside[q], piece, 0.0)
                if a == 7:
                    piece = jnp.where(lane < 4, vector, piece)
                packed[a, SLOTS.index(q)] = piece
            sends.append(pltpu.make_async_copy(packed.at[a], pieces.at[:, a], out_sems.at[a]))
            sends[-1].start()
    for send in sends:
        send.wait()


def pack(shifts, start, base, modes, control, target):
    hbm = pl.BlockSpec(memory_space=pltpu.HBM)
    f32 = jnp.float32
    return pl.pallas_call(
        pack_kernel,
        out_shape=jax.ShapeDtypeStruct((16, 8, 8, 128), f32),
        in_specs=[hbm] * 6,
        out_specs=hbm,
        scratch_shapes=[
            pltpu.VMEM((8, 8, 1536), f32),
            pltpu.VMEM((8, 16, 8, 128), f32),
            pltpu.SMEM((1, 4), f32),
            pltpu.SemaphoreType.DMA((5,)),
            pltpu.SemaphoreType.DMA((8,)),
            pltpu.SemaphoreType.DMA,
        ],
        compiler_params=pltpu.CompilerParams(vmem_limit_bytes=60 * 2**20),
    )(shifts, start, base, modes, control, target)


def spread_kernel(own, other, pieces, total):
    core = position()[2]
    total[...] = own[...] + other[...]
    lane = lax.broadcasted_iota(jnp.int32, (256, 128), 1)
    gradient = jnp.where(lane < CORE, total[...], 0.0)
    squares = jnp.sum(gradient * gradient, axis=(0, 1), keepdims=True)
    stats = pltpu.roll(total[:1], 64, 1)
    stats = jnp.where(lane[:1] < 2, stats, jnp.where(lane[:1] == 2, squares, 0.0))
    left = lane[:4] < CORE
    for q in range(16):
        rows = total[pl.ds(pl.multiple_of(16 * q + 8 * core, 8), 8), :]
        packed = jnp.where(left, rows[:4], pltpu.roll(rows[4:], 64, 1))
        for b in range(8):
            pieces[pl.ds(PIECE * (16 * b + q), 4), :] = packed
            pieces[pl.ds(PIECE * (16 * b + q) + 4, 1), :] = stats


def spread(own, other):
    vmem = pl.BlockSpec(memory_space=pltpu.VMEM)
    return pl.pallas_call(
        spread_kernel,
        out_shape=jax.ShapeDtypeStruct((128 * PIECE, 128), jnp.float32),
        in_specs=[vmem, vmem],
        out_specs=vmem,
        scratch_shapes=[pltpu.VMEM((256, 128), jnp.float32)],
        compiler_params=pltpu.CompilerParams(vmem_limit_bytes=8 * 2**20),
    )(own, other)


def finish_kernel(pieces, control, updated, objective):
    sums = [pieces[pl.ds(4 + i, 32, stride=4 * PIECE), :] for i in range(0, 4 * PIECE, PIECE)]
    stats = jnp.sum((sums[0] + sums[1]) + (sums[2] + sums[3]), axis=0, keepdims=True)
    lane = lax.broadcasted_iota(jnp.int32, (1, 128), 1)

    def entry(n):
        return jnp.sum(jnp.where(lane == n, stats, 0.0), axis=(0, 1), keepdims=True)

    cells = 256 * 8192
    objective[...] = (entry(0) * (0.5 / 32) + entry(1) * 0.25) / cells
    scaling = jnp.broadcast_to(0.5 / jnp.sqrt(entry(2) / cells + 1e-06), (4, 128))
    left = lax.broadcasted_iota(jnp.int32, (4, 128), 1) < CORE
    for n in range(64):
        columns = slice(128 * n, 128 * (n + 1))
        one, two = (pieces[pl.ds(PIECE * (2 * n + i), 4), :] for i in range(2))
        updated[:4, columns] = control[:4, columns] - scaling * jnp.where(left, one, pltpu.roll(two, 64, 1))
        updated[4:, columns] = control[4:, columns] - scaling * jnp.where(left, pltpu.roll(one, 64, 1), two)


def finish(pieces, control):
    vmem = pl.BlockSpec(memory_space=pltpu.VMEM)
    return pl.pallas_call(
        finish_kernel,
        out_shape=(jax.ShapeDtypeStruct((8, 8192), jnp.float32), jax.ShapeDtypeStruct((1, 1), jnp.float32)),
        in_specs=[vmem, vmem],
        out_specs=(vmem, vmem),
        compiler_params=pltpu.CompilerParams(vmem_limit_bytes=8 * 2**20),
    )(pieces, control)


def local(start_state, base_field, modes, control, target, shifts, gen_vector, point_ids):
    sent = pack(shifts, start_state, base_field, modes, control, target)
    own = lax.all_to_all(sent, LINKS, 0, 0, axis_index_groups=BLOCK_GROUPS, tiled=True)
    other = lax.ppermute(own, "slab", PAIRS)
    part = heat(gen_vector, point_ids, own, other)
    pieces = spread(part, lax.ppermute(part, "slab", PAIRS))
    pieces = pieces.reshape(128, 1, PIECE * 128)
    pieces = lax.all_to_all(pieces, LINKS, 0, 0, axis_index_groups=CORE_GROUPS, tiled=True)
    pieces = pieces.reshape(128 * PIECE, 128)
    new_control, objective = finish(pieces, control)
    return new_control, objective[0, 0]


def solution(mesh):
    return jax.shard_map(
        local,
        mesh=mesh,
        in_specs=(
            P("slab", None),
            P("slab", None),
            P(None, "slab", None),
            P("slab", None),
            P("slab", None),
            P("shift", None),
            P(),
            P(),
        ),
        out_specs=(P("slab", None), P()),
        check_vma=False,
    )
```

```python
import jax
import jax.numpy as jnp
from jax import lax
from jax.experimental import pallas as pl
from jax.experimental.pallas import tpu as pltpu
from jax.sharding import PartitionSpec as P

NLAT = 1021
HALF_DT = 0.02
DT = 0.04
HALO = 32
WIDE = 128
CORE = 64
LINES = 4
GROUP = 4
PIECE = 5
LINKS = ("shift", "slab")


X_OFF = (2, 1, 0, 1, 3, 2, 3, 0, 3, 0, 3, 2, 0, 1, 2, 1)
X_BITS = sum(x << (2 * q) for q, x in enumerate(X_OFF[:8])), sum(x << (2 * q) for q, x in enumerate(X_OFF[8:]))
SHIFT_ROWS = tuple(tuple(16 * (8 * c + X_OFF[8 * c : 8 * c + 8].index(x)) for x in range(4)) for c in range(2))


def position():
    shift, slab = lax.axis_index("shift"), lax.axis_index("slab")
    z_low, y, core = lax.div(slab, 8), lax.rem(lax.div(slab, 2), 4), lax.rem(slab, 2)
    z_high, x = lax.div(shift, 4), lax.rem(shift, 4)
    place = z_low * 4 + y
    bits = jnp.where(place < 8, X_BITS[0], X_BITS[1])
    offset = lax.rem(lax.shift_right_logical(bits, 2 * lax.rem(place, 8)), 4)
    block = lax.rem(z_high + 1 - lax.div(z_low, 2), 2) * 4 + lax.rem(x - offset + 4, 4)
    return block, place, core


def device_at(block, place, core):
    z_low, y = divmod(place, 4)
    z_high, x = divmod(block, 4)
    return ((z_high ^ (1 - z_low // 2)) * 4 + (x + X_OFF[place]) % 4) * 32 + z_low * 8 + y * 2 + core


BLOCK_GROUPS = [[device_at(b, q, c) for q in range(16)] for b in range(8) for c in range(2)]
CORE_GROUPS = [[device_at(b, q, c) for b in range(8) for q in range(16)] for c in range(2)]
PAIRS = [(i, i ^ 1) for i in range(32)]


def heat_kernel(gen, pts, own, other, part, tall, rows, horiz, ends, mid, cross, field, extra):
    lane = lax.broadcasted_iota(jnp.int32, (8, 128), 1)
    sub = lax.broadcasted_iota(jnp.int32, (8, 128), 0)
    half = lane >= 64
    block, place, core = position()
    strip = block * 16 + place

    for a in range(8):
        for q in range(16):
            tall[a, q, core] = own[q, a]
            tall[a, q, 1 - core] = other[q, a]
    flat = tall.reshape(8, 256, 128)
    zero = jnp.zeros((8, 128), jnp.float32)
    for i in range(LINES):
        field[0, i] = zero
        field[WIDE + 1, i] = zero
        horiz[WIDE, i] = zero

    scales = {1: HALF_DT, 6: DT, 7: -1.0}
    first_half = lax.broadcasted_iota(jnp.int32, (WIDE, 128), 1) < 64
    for a in (1, 2, 3, 4, 5, 6, 0, 7):
        for i in range(0, LINES, 2):
            pair = [flat[a, pl.ds(i + n, 64, stride=4), :] for n in range(2)]
            turned = jnp.concatenate(pair, axis=0).T
            if a in scales:
                turned = scales[a] * turned
            swapped = pltpu.roll(turned, 64, 1)
            rows[a, i] = jnp.where(first_half, turned, swapped)
            rows[a, i + 1] = jnp.where(first_half, swapped, turned)
            if a == 0:
                for n in range(2):
                    rows[a, i + n] += rows[6, i + n]

    weights = []
    for k in range(4):
        product = [lax.rem(pts[p] * gen[k], NLAT).astype(jnp.float32) / NLAT for p in range(4)]
        value = jnp.where(sub % 4 == 0, product[0], jnp.where(sub % 4 == 1, product[1], jnp.where(sub % 4 == 2, product[2], product[3])))
        found = []
        for y in range(4):
            line = flat[7, pl.ds(jnp.where(core == 0, SHIFT_ROWS[0][y], SHIFT_ROWS[1][y]), 1), :]
            found.append(jnp.broadcast_to(line[:, k : k + 1], (8, 128)))
        shift = jnp.where(half, jnp.where(sub < 4, found[2], found[3]), jnp.where(sub < 4, found[0], found[1]))
        value = value + shift
        value = value - jnp.floor(value)
        weights.append(0.5 - jnp.abs(2.0 * value - 1.0))

    def row(a, i, k):
        return jnp.broadcast_to(rows[a, i, pl.ds(k, 1), :], (8, 128))

    top = lane % 64 == 0
    bottom = lane % 64 == 63

    def coefs_at(k, left):
        c = []
        for i in range(LINES):
            e = (weights[0] * row(2, i, k) + weights[1] * row(3, i, k)) + (weights[2] * row(4, i, k) + weights[3] * row(5, i, k))
            c.append(row(1, i, k) * jnp.exp(e))
            horiz[k, i] = left[i] + c[i]
            field[k + 1, i] = row(0, i, k)
        for i in range(3):
            mid[k, i] = c[i] + c[i + 1]
        over, under = pltpu.roll(c[3], 1, 1), pltpu.roll(c[0], 127, 1)
        cross[k, 0] = jnp.where(top, 0.0, c[0] + over)
        cross[k, 1] = jnp.where(bottom, 0.0, c[3] + under)
        ends[k, 0] = 1.0 - jnp.where(top, c[0], c[0] + over)
        ends[k, 1] = 1.0 - jnp.where(bottom, c[3], c[3] + under)
        return tuple(c)

    lax.fori_loop(0, WIDE, coefs_at, (zero,) * LINES, unroll=32)

    def load(k):
        return tuple(field[k + 1, i] for i in range(LINES))

    def flux(k, u, right):
        return tuple(horiz[k + 1, i] * (right[i] - u[i]) for i in range(LINES))

    keep = {
        HALO - 1: jnp.where(strip == 0, 0.0, 1.0).astype(jnp.float32),
        WIDE - HALO: jnp.where(strip == 127, 0.0, 1.0).astype(jnp.float32),
    }

    def sweep(low, source, save):
        u = load(low)
        before = flux(low - 1, load(low - 1), u)
        for k in range(low, WIDE - low):
            right = load(k + 1)
            after = flux(k, u, right)
            down = [mid[k, i] * (u[i + 1] - u[i]) for i in range(3)]
            over, under = cross[k, 0] * pltpu.roll(u[3], 1, 1), cross[k, 1] * pltpu.roll(u[0], 127, 1)
            for i in range(LINES):
                y = (after[i] - before[i]) + (u[i] if 0 < i < 3 else ends[k, i // 3] * u[i])
                if source is not None:
                    y = y + source(k, i)
                y = y + (down[i] if i < 3 else under)
                y = y - down[i - 1] if i else y + over
                if k in keep:
                    y = y * keep[k]
                field[k + 1, i] = y
                if save:
                    extra[k, i] = y
            before, u = after, right

    def steps(first, last, source, save=False):
        while first <= last:
            times = min(GROUP, last - first + 1)

            def one(_, c, low=first):
                sweep(low, source, save)
                return c

            lax.fori_loop(0, times, one, 0)
            first += times

    control = lambda k, i: row(6, i, k)
    target = lambda k, i: row(7, i, k)
    misfit = lambda k, i: extra[k, i]

    steps(1, 15, control)
    steps(16, 16, target, True)

    def add_loss(k, total):
        return tuple(total[i] + extra[k, i] * extra[k, i] for i in range(LINES))

    loss = lax.fori_loop(HALO, HALO + CORE, add_loss, (zero,) * LINES, unroll=64)
    loss = jnp.sum((loss[0] + loss[1]) + (loss[2] + loss[3]), axis=(0, 1), keepdims=True)
    last = 16
    for power in (8, 4, 2, 1):
        steps(last + 1, last + power - 1, None)
        last += power
        steps(last, last, misfit, power > 1)
    steps(32, 32, None)

    inner = flat[6, :, HALO : HALO + CORE]
    squares = 0.5 * jnp.sum(inner * inner, axis=(0, 1), keepdims=True)
    wide_lane = lax.broadcasted_iota(jnp.int32, (256, CORE), 1)
    part[:, CORE:] = jnp.where(wide_lane == 0, loss, jnp.where(wide_lane == 1, squares, 0.0))
    part[:, :CORE] = 0.25 * inner
    for i in range(LINES):
        total = jnp.sum(field[pl.ds(HALO + 1, CORE), i], axis=1)
        total = (total + pltpu.roll(total, 64, 1)) * (DT / 32)
        part[pl.ds(i, 64, stride=4), :] += jnp.concatenate([total.T[:64], jnp.zeros((64, CORE), jnp.float32)], axis=1)


def heat(gen, pts, own, other):
    smem = pl.BlockSpec(memory_space=pltpu.SMEM)
    vmem = pl.BlockSpec(memory_space=pltpu.VMEM)
    f32 = jnp.float32
    return pl.pallas_call(
        heat_kernel,
        out_shape=jax.ShapeDtypeStruct((256, 128), f32),
        in_specs=[smem, smem, vmem, vmem],
        out_specs=vmem,
        scratch_shapes=[
            pltpu.VMEM((8, 16, 2, 8, 128), f32),
            pltpu.VMEM((8, LINES, WIDE, 128), f32),
            pltpu.VMEM((WIDE + 1, LINES, 8, 128), f32),
            pltpu.VMEM((WIDE, 2, 8, 128), f32),
            pltpu.VMEM((WIDE, 3, 8, 128), f32),
            pltpu.VMEM((WIDE, 2, 8, 128), f32),
            pltpu.VMEM((WIDE + 2, LINES, 8, 128), f32),
            pltpu.VMEM((WIDE, LINES, 8, 128), f32),
        ],
        compiler_params=pltpu.CompilerParams(vmem_limit_bytes=48 * 2**20),
    )(gen, pts, own, other)


def pack_kernel(shifts, start, base, modes, control, target, pieces, window, packed, vector_of, sems, out_sems, shift_sem):
    block = position()[0]
    shift_copy = pltpu.make_async_copy(shifts, vector_of, shift_sem)
    shift_copy.start()
    column = block * 1024
    begin = pl.multiple_of(jnp.clip(column - 128, 0, 8192 - 1280), 128)
    ahead = pl.multiple_of(column - begin, 128)
    sources = ((start, 0), (base, 1), (control, 6), (target, 7), (modes, slice(2, 6)))
    copies = []
    for n, (source, a) in enumerate(sources):
        copy = pltpu.make_async_copy(source.at[..., pl.ds(begin, 1280)], window.at[a, :, 128:1408], sems.at[n])
        copy.start()
        copies.append(copy)
    shift_copy.wait()
    lane = lax.broadcasted_iota(jnp.int32, (8, 128), 1)
    vector = jnp.zeros((8, 128), jnp.float32)
    for m in range(4):
        vector = jnp.where(lane == m, vector_of[0, m], vector)
    inside = {
        0: jnp.logical_or(lane >= HALO, block > 0),
        15: jnp.logical_or(lane < WIDE - HALO, block < 7),
    }
    sends = []
    for group, arrays in zip(copies, ((0,), (1,), (6,), (7,), (2, 3, 4, 5))):
        group.wait()
        for a in arrays:
            for q in range(16):
                two = window[a, :, pl.ds(pl.multiple_of(ahead + 128 * ((q + 1) // 2), 128), 256)]
                piece = two[:, 32:160] if q % 2 else two[:, 96:224]
                if q in inside:
                    piece = jnp.where(inside[q], piece, 0.0)
                if a == 7:
                    piece = jnp.where(lane < 4, vector, piece)
                packed[a, q] = piece
            sends.append(pltpu.make_async_copy(packed.at[a], pieces.at[:, a], out_sems.at[a]))
            sends[-1].start()
    for send in sends:
        send.wait()


def pack(shifts, start, base, modes, control, target):
    hbm = pl.BlockSpec(memory_space=pltpu.HBM)
    f32 = jnp.float32
    return pl.pallas_call(
        pack_kernel,
        out_shape=jax.ShapeDtypeStruct((16, 8, 8, 128), f32),
        in_specs=[hbm] * 6,
        out_specs=hbm,
        scratch_shapes=[
            pltpu.VMEM((8, 8, 1536), f32),
            pltpu.VMEM((8, 16, 8, 128), f32),
            pltpu.SMEM((1, 4), f32),
            pltpu.SemaphoreType.DMA((5,)),
            pltpu.SemaphoreType.DMA((8,)),
            pltpu.SemaphoreType.DMA,
        ],
        compiler_params=pltpu.CompilerParams(vmem_limit_bytes=60 * 2**20),
    )(shifts, start, base, modes, control, target)


def spread_kernel(own, other, pieces, total):
    core = position()[2]
    total[...] = own[...] + other[...]
    lane = lax.broadcasted_iota(jnp.int32, (256, 128), 1)
    gradient = jnp.where(lane < CORE, total[...], 0.0)
    squares = jnp.sum(gradient * gradient, axis=(0, 1), keepdims=True)
    stats = pltpu.roll(total[:1], 64, 1)
    stats = jnp.where(lane[:1] < 2, stats, jnp.where(lane[:1] == 2, squares, 0.0))
    left = lane[:4] < CORE
    for q in range(16):
        rows = total[pl.ds(pl.multiple_of(16 * q + 8 * core, 8), 8), :]
        packed = jnp.where(left, rows[:4], pltpu.roll(rows[4:], 64, 1))
        for b in range(8):
            pieces[pl.ds(PIECE * (16 * b + q), 4), :] = packed
            pieces[pl.ds(PIECE * (16 * b + q) + 4, 1), :] = stats


def spread(own, other):
    vmem = pl.BlockSpec(memory_space=pltpu.VMEM)
    return pl.pallas_call(
        spread_kernel,
        out_shape=jax.ShapeDtypeStruct((128 * PIECE, 128), jnp.float32),
        in_specs=[vmem, vmem],
        out_specs=vmem,
        scratch_shapes=[pltpu.VMEM((256, 128), jnp.float32)],
        compiler_params=pltpu.CompilerParams(vmem_limit_bytes=8 * 2**20),
    )(own, other)


def finish_kernel(pieces, control, updated, objective):
    sums = [pieces[pl.ds(4 + i, 32, stride=4 * PIECE), :] for i in range(0, 4 * PIECE, PIECE)]
    stats = jnp.sum((sums[0] + sums[1]) + (sums[2] + sums[3]), axis=0, keepdims=True)
    lane = lax.broadcasted_iota(jnp.int32, (1, 128), 1)

    def entry(n):
        return jnp.sum(jnp.where(lane == n, stats, 0.0), axis=(0, 1), keepdims=True)

    cells = 256 * 8192
    objective[...] = (entry(0) * (0.5 / 32) + entry(1) * 0.25) / cells
    scaling = jnp.broadcast_to(0.5 / jnp.sqrt(entry(2) / cells + 1e-06), (4, 128))
    left = lax.broadcasted_iota(jnp.int32, (4, 128), 1) < CORE
    for n in range(64):
        columns = slice(128 * n, 128 * (n + 1))
        one, two = (pieces[pl.ds(PIECE * (2 * n + i), 4), :] for i in range(2))
        updated[:4, columns] = control[:4, columns] - scaling * jnp.where(left, one, pltpu.roll(two, 64, 1))
        updated[4:, columns] = control[4:, columns] - scaling * jnp.where(left, pltpu.roll(one, 64, 1), two)


def finish(pieces, control):
    vmem = pl.BlockSpec(memory_space=pltpu.VMEM)
    return pl.pallas_call(
        finish_kernel,
        out_shape=(jax.ShapeDtypeStruct((8, 8192), jnp.float32), jax.ShapeDtypeStruct((1, 1), jnp.float32)),
        in_specs=[vmem, vmem],
        out_specs=(vmem, vmem),
        compiler_params=pltpu.CompilerParams(vmem_limit_bytes=8 * 2**20),
    )(pieces, control)


def local(start_state, base_field, modes, control, target, shifts, gen_vector, point_ids):
    sent = pack(shifts, start_state, base_field, modes, control, target)
    own = lax.all_to_all(sent, LINKS, 0, 0, axis_index_groups=BLOCK_GROUPS, tiled=True)
    other = lax.ppermute(own, "slab", PAIRS)
    part = heat(gen_vector, point_ids, own, other)
    pieces = spread(part, lax.ppermute(part, "slab", PAIRS))
    pieces = pieces.reshape(128, 1, PIECE * 128)
    pieces = lax.all_to_all(pieces, LINKS, 0, 0, axis_index_groups=CORE_GROUPS, tiled=True)
    pieces = pieces.reshape(128 * PIECE, 128)
    new_control, objective = finish(pieces, control)
    return new_control, objective[0, 0]


def solution(mesh):
    return jax.shard_map(
        local,
        mesh=mesh,
        in_specs=(
            P("slab", None),
            P("slab", None),
            P(None, "slab", None),
            P("slab", None),
            P("slab", None),
            P("shift", None),
            P(),
            P(),
        ),
        out_specs=(P("slab", None), P()),
        check_vma=False,
    )
```
